256 devices in a mesh: row: 32 (over z_lo, y, core), col: 8 (over z_hi, x).
Axes of the slice: x: 4, y: 4, z: 8 (z_hi: 2, z_lo: 4; z = z_hi * 4 + z_lo), core: 2. Of those that a mesh axis runs over, the one named last changes fastest.
Arguments:
- queries: bfloat16 [256, 32, 3072], P('row', None, 'col'), may hold values from -50 to 50
- keys: bfloat16 [256, 32, 3072], P('row', None, 'col'), may hold values from -6 to 6
- values: bfloat16 [256, 32, 3072], P('row', None, 'col'), may hold values from -6 to 6
- out_grad: bfloat16 [256, 32, 3072], P('row', None, 'col'), may hold values from -6 to 6
- outputs: bfloat16 [256, 32, 3072], P('row', None, 'col'), may hold values from -6 to 6
- bias: bfloat16 [3072, 3072], P('row', 'col'), may hold values from -6 to 6
- key_mask: int32 [3072], P('col'), may hold values 0 or 1
Outputs:
- query_grad: bfloat16 [256, 32, 3072], P('row', None, 'col')
- key_grad: bfloat16 [256, 32, 3072], P('row', None, 'col')
- value_grad: bfloat16 [256, 32, 3072], P('row', None, 'col')
- bias_grad: float32 [3072, 3072], P('row', 'col')
The draws below stay inside these ranges and needn't reach their ends.
All inputs are finite; a program needn't handle non-finite values. No bound on the sum of `key_mask` on one device may be relied on, other than what follows from the above.
Results may differ from the reference program's by a relative error of at most 0.005.
Values may be sent and summed in bfloat16 or wider, within the bound.
No kernel may reach another device: no remote copies, remote signals or barrier semaphores. Data moves between devices by JAX's collectives and lax.ppermute only.
A program may use at most 128 MiB of HBM per device.

```python
import jax
import jax.numpy as jnp
from jax import lax

HEAD = 32
NTOK = 3072
ROWS = 256


def draw_keys(key, part):
    key = jax.random.fold_in(key, 3)
    return jnp.clip(jax.random.normal(key, (ROWS, HEAD, NTOK), jnp.float32), -6.0, 6.0).astype(jnp.bfloat16)


def draw_queries(key, part):
    key = jax.random.fold_in(key, 5)
    return jnp.clip(jax.random.normal(key, (ROWS, HEAD, NTOK), jnp.float32), -6.0, 6.0).astype(jnp.bfloat16)


def touch_ends(entries, stream_key, low, top_value):
    spot = [jax.random.randint(jax.random.fold_in(stream_key, axis), (), 0, length) for axis, length in enumerate(entries.shape)]
    widest = entries.shape.index(max(entries.shape))
    next_to = spot[:widest] + [(spot[widest] + 1) % entries.shape[widest]] + spot[widest + 1:]
    return entries.at[tuple(spot)].set(low).at[tuple(next_to)].set(top_value)


def strengthened(drawn, stream_key, source, target, shards_of, factor):
    owner, partner = [(jnp.arange(drawn.shape[axis_at]) // (drawn.shape[axis_at] // shards_of)).reshape([-1 if axis == axis_at else 1 for axis in range(drawn.ndim)]) for axis_at in (source, target)]
    chosen = jax.random.permutation(stream_key, shards_of)[partner]
    strong = (owner == chosen) | (owner == (partner + shards_of // 2) % shards_of)
    return jnp.where(strong, factor * drawn, drawn)


def shard_levels(stream_key, extent, cuts, least, top_value):
    loudness, own = 1.0, jax.random.fold_in(stream_key, 6)
    for axis_at, blocks in cuts:
        draws = jnp.exp(jax.random.uniform(jax.random.fold_in(own, axis_at), (blocks,), jnp.float32, least / len(cuts), top_value / len(cuts)))
        loudness = loudness * jnp.repeat(draws, extent[axis_at] // blocks).reshape([-1 if axis == axis_at else 1 for axis in range(len(extent))])
    return loudness


def scatter_about(key, extent, scale, limit, pieces=(), kind=jnp.bfloat16):
    entries = jax.random.normal(key, extent, jnp.float32) * scale
    if len(pieces) > 0:
        entries = shard_levels(key, extent, pieces, -0.22, 0.18) * entries
    return jnp.clip(entries, min=-limit, max=limit).astype(kind)


def noise_with(own_key, extent, width, limit, pieces, heavy, held_as=jnp.bfloat16):
    array = width * jax.random.normal(own_key, extent, jnp.float32)
    if pieces:
        array = array * shard_levels(own_key, extent, pieces, -0.22, 0.18)
    return jnp.clip(strengthened(array, jax.random.fold_in(own_key, 3), *heavy), -limit, limit).astype(held_as)


def setup_inputs(seed: int = 0) -> dict:
    key_list = jax.random.split(jax.random.key(seed), 8)
    queries = draw_queries(jax.random.fold_in(key_list[7], 71), 0)
    keys = draw_keys(jax.random.fold_in(key_list[7], 71), 0)
    values = scatter_about(key_list[2], (ROWS, HEAD, NTOK), 1.0, 6.0, ((0, 32), (2, 8)))
    out_grad = noise_with(key_list[3], (ROWS, HEAD, NTOK), 1.0, 6.0, ((0, 32), (2, 8)), (0, 2, 32, 2.75))
    outputs = scatter_about(key_list[4], (ROWS, HEAD, NTOK), 1.0, 6.0, ((0, 32), (2, 8)))
    bias = scatter_about(key_list[5], (NTOK, NTOK), 1.0, 6.0, ((0, 32), (1, 8)))
    key_mask = touch_ends((jax.random.randint(key_list[6], (NTOK,), 0, 8) < 7).astype(jnp.int32), jax.random.fold_in(key_list[6], 1), 0, 1)
    return dict(queries=queries, keys=keys, values=values, out_grad=out_grad, outputs=outputs, bias=bias, key_mask=key_mask)


def reference(queries, keys, values, out_grad, outputs, bias, key_mask):
    scale = HEAD ** -0.5
    offset = jnp.where(key_mask == 0, -1e9, 0.0).astype(jnp.float32)
    full_bias = bias.astype(jnp.float32) + offset[None, :]

    def one_row(acc, parts):
        query, keyrow, valrow, gradrow, outrow = parts
        qf = query.astype(jnp.float32)
        kf = keyrow.astype(jnp.float32)
        gf = gradrow.astype(jnp.float32)
        scores = jnp.einsum('cj,ct->jt', qf, kf) * scale + full_bias
        top = jnp.max(scores, axis=1)
        lse = top + jnp.log(jnp.sum(jnp.exp(scores - top[:, None]), axis=1))
        probs = jnp.exp(scores - lse[:, None])
        probs_low = probs.astype(jnp.bfloat16)
        delta = jnp.sum(gf * outrow.astype(jnp.float32), axis=0)
        dprobs = jnp.einsum('cj,ct->jt', gf, valrow.astype(jnp.float32))
        dscores = probs * (dprobs - delta[:, None])
        dscores_low = dscores.astype(jnp.bfloat16).astype(jnp.float32)
        value_grad = jnp.einsum('jt,cj->ct', probs_low.astype(jnp.float32), gf).astype(jnp.bfloat16)
        key_grad = (scale * jnp.einsum('jt,cj->ct', dscores_low, qf)).astype(jnp.bfloat16)
        query_grad = (scale * jnp.einsum('jt,ct->cj', dscores_low, kf)).astype(jnp.bfloat16)
        return acc + dscores, (query_grad, key_grad, value_grad)

    start = jnp.zeros((NTOK, NTOK), jnp.float32)
    bias_grad, (query_grad, key_grad, value_grad) = lax.scan(
        one_row, start, (queries, keys, values, out_grad, outputs))
    return query_grad, key_grad, value_grad, bias_grad
```

```python
import math

import jax
import jax.numpy as jnp
from jax import lax
from jax.experimental import pallas as pl
from jax.experimental.pallas import tpu as pltpu
from jax.sharding import Mesh, PartitionSpec as P

FINE = ("zlo", "y", "core", "zhi", "x")
ZLO, Y, CORE, ZHI, X = 4, 4, 2, 2, 4
LOG2E = math.log2(math.e)
MASKED = -8192.0
BF16, F32 = jnp.bfloat16, jnp.float32


def dot(a, b, ca, cb):
    return lax.dot_general(a, b, (((ca,), (cb,)), ((), ())), preferred_element_type=F32)


def split3(x):
    high = x.astype(BF16).astype(F32)
    rest = x - high
    middle = rest.astype(BF16).astype(F32)
    return high, middle, rest - middle


def rows_of(parts, count, width):
    row = lax.broadcasted_iota(jnp.int32, (count, width), 0)
    out = jnp.zeros((count, width), F32)
    for at, part in enumerate(parts):
        out = jnp.where(row == at, part, out)
    return out


def put_keys(refs, masks, place, scale):
    rows, head, width = refs[0].shape
    for slot, (ref, mask) in enumerate(zip(refs, masks)):
        offset = jnp.where(mask[...] == 0.0, MASKED, 0.0)
        extra = rows_of((-1.0, -1.0, -1.0, offset), head, width)

        def prepare(i, carry):
            parts = split3(ref[i].astype(F32) * scale)
            whole = jnp.concatenate(parts + (extra,), axis=0)
            place[i, slot * width : (slot + 1) * width, :] = whole.T.astype(BF16)
            return carry

        lax.fori_loop(0, rows, prepare, 0)


def put_values(refs, place):
    rows, head, width = refs[0].shape
    extra = rows_of((-1.0, -1.0, -1.0), 128 - head, width)
    for slot, ref in enumerate(refs):

        def prepare(i, carry):
            whole = jnp.concatenate((ref[i].astype(F32), extra), axis=0)
            place[i, slot * width : (slot + 1) * width, :] = whole.T.astype(BF16)
            return carry

        lax.fori_loop(0, rows, prepare, 0)


def bias_pieces(at):
    zlo, y, core, zhi, x = (at[n] for n in range(5))
    for yd in range(Y):
        row = lax.rem(y + yd, Y)
        for zd in range(ZLO):
            piece = lax.rem(zlo + zd, ZLO)
            half, part = lax.div(piece, 2), lax.rem(piece, 2)
            slot = lax.rem(half + zhi, 2)
            chunk = lax.rem(part * 2 + lax.div(row, 2) - x + X, X)
            for other in range(CORE):
                which = lax.rem(core + other, 2)
                first = chunk * 384 + lax.rem(row, 2) * 192 + which * 96
                yield yd, zd, other, slot, pl.multiple_of(first, 32)


def stats_kernel(scale, at, *refs):
    q = refs[0:4]
    keys, masks = refs[4:6], refs[6:8]
    grad, outs = refs[8:10]
    pieces = (refs[10:14], refs[14:18])
    stat, bias_t = refs[18:20]
    bias_n, bias_f, key_t = refs[20:]
    rows, head, width = q[0].shape
    total = X * width
    put_keys(keys, masks, key_t, scale * LOG2E)
    for yd, zd, other, slot, first in bias_pieces(at):
        bias_n[slot, pl.ds(first, 96), :] = pieces[other][yd][zd]
    for slot in range(2):
        for j in range(0, total, 128):
            tile = bias_n[slot, j : j + 128, :].astype(F32).T
            bias_t[slot * width : (slot + 1) * width, j : j + 128] = tile.astype(BF16)
            bias_f[slot * width : (slot + 1) * width, j : j + 128] = tile * LOG2E
    ones = rows_of((0.0, 0.0, 0.0, 1.0), 16, width).astype(BF16)

    def row_step(i, carry):
        for d in range(X):
            query = q[d][i]
            augmented = jnp.concatenate((query, query, query, ones), axis=0)
            cols = slice(d * width, (d + 1) * width)
            top, total_sum = None, None
            for k in range(0, 2 * width, 128):
                scores = dot(key_t[i, k : k + 128, :112], augmented, 1, 0)
                scores = (scores + bias_f[k : k + 128, cols]).reshape(16, 8, width)
                here = jnp.max(scores, axis=0)
                if top is None:
                    top = here
                    total_sum = jnp.sum(jnp.exp2(scores - top), axis=0)
                else:
                    new = jnp.maximum(top, here)
                    total_sum = total_sum * jnp.exp2(top - new) + jnp.sum(
                        jnp.exp2(scores - new), axis=0
                    )
                    top = new
            most = jnp.max(top, axis=0, keepdims=True)
            summed = jnp.sum(total_sum * jnp.exp2(top - most), axis=0, keepdims=True)
            stat[pl.ds(i, 1), cols] = most
            stat[pl.ds(i, 1), total + d * width : total + (d + 1) * width] = summed
        product = grad[i].astype(F32) * outs[i].astype(F32)
        stat[pl.ds(i, 1), 2 * total :] = jnp.sum(product, axis=0, keepdims=True)
        return carry

    lax.fori_loop(0, rows, row_step, 0)


def main_kernel(scale, at, *refs):
    q, g = refs[0:4], refs[4:8]
    keys, values, masks = refs[8:10], refs[10:12], refs[12:14]
    stats = refs[14:18]
    bias_t = refs[18]
    dq = refs[19:23]
    dk_own, dv_own, dkv_away = refs[23:26]
    bias_own, bias_away = refs[26:30], refs[30:34]
    bias_f, acc, turned, key_t, value_t, lse, delta = refs[34:]
    rows, head, width = q[0].shape
    total = X * width
    put_keys(keys, masks, key_t, scale * LOG2E)
    put_values(values, value_t)
    for d in range(X):
        cols = slice(d * width, (d + 1) * width)
        there = [(d - e) % X for e in range(X)]
        tops = [stats[e][:, n * width : (n + 1) * width] for e, n in enumerate(there)]
        sums = [stats[e][:, total + n * width : total + (n + 1) * width] for e, n in enumerate(there)]
        top = jnp.maximum(jnp.maximum(tops[0], tops[1]), jnp.maximum(tops[2], tops[3]))
        summed = sum(s * jnp.exp2(t - top) for s, t in zip(sums, tops))
        lse[:, cols] = top + jnp.log(summed) * LOG2E
        delta[:, cols] = stats[d][:, 2 * total :]
    bias_f[...] = bias_t[...].astype(F32) * LOG2E
    acc[...] = jnp.zeros_like(acc)

    def row_step(i, carry):
        dk_row, dv_row = None, None
        for d in range(X):
            cols = slice(d * width, (d + 1) * width)
            query, gradient = q[d][i], g[d][i]
            high, middle, low = split3(lse[pl.ds(i, 1), cols])
            extra = rows_of((high, middle, low, 1.0), 16, width).astype(BF16)
            query_all = jnp.concatenate((query, query, query, extra), axis=0)
            extra = rows_of(split3(delta[pl.ds(i, 1), cols]), 16, width).astype(BF16)
            gradient_all = jnp.concatenate((gradient, extra), axis=0)
            probs = jnp.exp2(dot(key_t[i, :, :112], query_all, 1, 0) + bias_f[:, cols])
            dscores = probs * dot(value_t[i, :, :48], gradient_all, 1, 0)
            acc[:, cols] += dscores
            probs_low, dscores_low = probs.astype(BF16), dscores.astype(BF16)
            dv_part = dot(gradient, probs_low, 1, 1)
            dk_part = dot(query, dscores_low, 1, 1)
            dv_row = dv_part if d == 0 else dv_row + dv_part
            dk_row = dk_part if d == 0 else dk_row + dk_part
            dq_part = dot(keys[0][i], dscores_low[:width], 1, 0) + dot(
                keys[1][i], dscores_low[width:], 1, 0
            )
            dq[d][i] = dq_part.astype(dq[d].dtype)
        dk_own[i], dv_own[i] = dk_row[:, :width], dv_row[:, :width]
        dkv_away[i] = dk_row[:, width:].astype(BF16)
        dkv_away[rows + i] = dv_row[:, width:].astype(BF16)
        return carry

    lax.fori_loop(0, rows, row_step, 0)
    for slot in range(2):
        for j in range(0, total, 128):
            tile = acc[slot * width : (slot + 1) * width, j : j + 128].T
            turned[slot, j : j + 128, :] = tile
    for yd, zd, other, slot, first in bias_pieces(at):
        place = bias_own if other == 0 else bias_away
        place[yd][zd] = turned[slot, pl.ds(first, 96), :].astype(place[yd].dtype)


VMEM = pl.BlockSpec(memory_space=pltpu.VMEM)
SMEM = pl.BlockSpec(memory_space=pltpu.SMEM)


def call(kernel, name, args, outs, scratch):
    return pl.pallas_call(
        kernel,
        in_specs=[SMEM] + [VMEM] * (len(args) - 1),
        out_specs=[VMEM] * len(outs),
        out_shape=[jax.ShapeDtypeStruct(shape, dtype) for shape, dtype in outs],
        scratch_shapes=[pltpu.VMEM(shape, dtype) for shape, dtype in scratch],
        compiler_params=pltpu.CompilerParams(vmem_limit_bytes=52 * 2**20),
        name=name,
    )(*args)


def fetch(x, axis, size, distance):
    return lax.ppermute(x, axis, [((n + distance) % size, n) for n in range(size)])


def deliver(x, axis, size, distance):
    return lax.ppermute(x, axis, [(n, (n + distance) % size) for n in range(size)])


def z_pairs(distance):
    pairs = []
    for group in range(ZHI):
        for place in range(ZLO):
            half, part = divmod((place + distance) % ZLO, 2)
            pairs.append(((2 * group + part) * ZHI + half, place * ZHI + group))
    return pairs


def per_device(queries, keys, values, out_grad, outputs, bias, key_mask):
    rows, head, width = keys.shape
    scale = head ** (-0.5)
    total = X * width
    z_axes = ("zlo", "zhi")
    at = jnp.stack([lax.axis_index(name) for name in FINE]).astype(jnp.int32)
    mask = key_mask.astype(F32)[None, :]

    from_z = jnp.stack([lax.ppermute(bias, z_axes, z_pairs(d)) for d in range(ZLO)])
    q = [queries] + [fetch(queries, "x", X, d) for d in range(1, X)]
    away = [fetch(a, "zhi", ZHI, 1) for a in (keys, values, mask)]
    here = [from_z] + [fetch(from_z, "y", Y, d) for d in range(1, Y)]
    there = [fetch(a, "core", CORE, 1) for a in here]
    g = [out_grad] + [fetch(out_grad, "x", X, d) for d in range(1, X)]

    both = 2 * width
    stat, bias_t = call(
        lambda *refs: stats_kernel(scale, *refs),
        "softmax_statistics",
        [at, *q, keys, away[0], mask, away[2], out_grad, outputs, *here, *there],
        [((rows, 2 * total + width), F32), ((both, total), BF16)],
        [((2, total, width), BF16), ((both, total), F32), ((rows, both, 128), BF16)],
    )
    stats = [stat] + [fetch(stat, "x", X, d) for d in range(1, X)]

    block, piece = (rows, head, width), (ZLO, 96, width)
    results = call(
        lambda *refs: main_kernel(scale, *refs),
        "attention_gradients",
        [at, *q, *g, keys, away[0], values, away[1], mask, away[2], *stats, bias_t],
        [(block, F32)]
        + [(block, BF16)] * 3
        + [(block, F32)] * 2
        + [((2 * rows, head, width), BF16)]
        + [(piece, F32)] * 4
        + [(piece, BF16)] * 4,
        [
            ((both, total), F32),
            ((both, total), F32),
            ((2, total, width), F32),
            ((rows, both, 128), BF16),
            ((rows, both, 128), BF16),
            ((rows, total), F32),
            ((rows, total), F32),
        ],
    )
    dq, (dk, dv, dkv_away) = results[0:4], results[4:7]
    bias_own, bias_away = results[7:11], results[11:15]

    near = [
        own + fetch(other, "core", CORE, 1).astype(F32)
        for own, other in zip(bias_own, bias_away)
    ]
    along_y = near[0]
    for d in range(1, Y):
        along_y = along_y + deliver(near[d].astype(BF16), "y", Y, d).astype(F32)
    low = along_y.astype(BF16)
    bias_grad = None
    for d in range(ZLO):
        pairs = [(worker, owner) for owner, worker in z_pairs(d)]
        part = lax.ppermute(low[d], z_axes, pairs).astype(F32)
        bias_grad = part if bias_grad is None else bias_grad + part

    query_sum = dq[0]
    for d in range(1, X):
        query_sum = query_sum + deliver(dq[d], "x", X, d).astype(F32)
    arrived = fetch(dkv_away, "zhi", ZHI, 1).astype(F32)
    query_grad = (scale * query_sum).astype(BF16)
    key_grad = (scale * (dk + arrived[:rows])).astype(BF16)
    value_grad = (dv + arrived[rows:]).astype(BF16)
    return query_grad, key_grad, value_grad, bias_grad


def solution(mesh):
    fine = Mesh(mesh.devices.reshape(ZLO, Y, CORE, ZHI, X), FINE)
    row, col = ("zlo", "y", "core"), ("zhi", "x")
    pair, flat = P(row, None, col), P(row, col)
    return jax.shard_map(
        per_device,
        mesh=fine,
        in_specs=(pair,) * 5 + (flat, P(col)),
        out_specs=(pair,) * 3 + (flat,),
        check_vma=False,
    )
```

```python
import math

import jax
import jax.numpy as jnp
from jax import lax
from jax.experimental import pallas as pl
from jax.experimental.pallas import tpu as pltpu
from jax.sharding import Mesh, PartitionSpec as P

FINE = ("zlo", "y", "core", "zhi", "x")
ZLO, Y, CORE, ZHI, X = 4, 4, 2, 2, 4
LOG2E = math.log2(math.e)
MASKED = -8192.0
BF16, F32 = jnp.bfloat16, jnp.float32


def dot(a, b, ca, cb):
    return lax.dot_general(a, b, (((ca,), (cb,)), ((), ())), preferred_element_type=F32)


def split3(x):
    high = x.astype(BF16).astype(F32)
    rest = x - high
    middle = rest.astype(BF16).astype(F32)
    return high, middle, rest - middle


def rows_of(parts, count, width):
    row = lax.broadcasted_iota(jnp.int32, (count, width), 0)
    out = jnp.zeros((count, width), F32)
    for at, part in enumerate(parts):
        out = jnp.where(row == at, part, out)
    return out


def put_keys(refs, masks, place, scale):
    rows, head, width = refs[0].shape
    for slot, (ref, mask) in enumerate(zip(refs, masks)):
        offset = jnp.where(mask == 0.0, MASKED, 0.0)
        extra = rows_of((-1.0, -1.0, -1.0, offset), head, width)

        def prepare(i, carry):
            parts = split3(ref[i].astype(F32) * scale)
            whole = jnp.concatenate(parts + (extra,), axis=0)
            place[i, slot * width : (slot + 1) * width, :] = whole.T.astype(BF16)
            return carry

        lax.fori_loop(0, rows, prepare, 0)


def put_values(refs, place):
    rows, head, width = refs[0].shape
    extra = rows_of((-1.0, -1.0, -1.0), 128 - head, width)
    for slot, ref in enumerate(refs):

        def prepare(i, carry):
            whole = jnp.concatenate((ref[i].astype(F32), extra), axis=0)
            place[i, slot * width : (slot + 1) * width, :] = whole.T.astype(BF16)
            return carry

        lax.fori_loop(0, rows, prepare, 0)


def bias_pieces(at, half):
    zlo, y, core, zhi, x = (at[n] for n in range(5))
    for yd in range(Y):
        row = lax.rem(y + yd, Y)
        for key_half in range(ZHI):
            zd = lax.rem(key_half * 2 + half - zlo + ZLO, ZLO)
            slot = lax.rem(key_half + zhi, 2)
            for other in range(CORE):
                which = lax.rem(core + other, 2)
                first = pl.multiple_of(row * 192 + which * 96, 32)
                yield yd, key_half, zd, other, slot, first


def stats_kernel(scale, half, at, *refs):
    both_qg, keys, away, mask = refs[0:4]
    pieces = (refs[4:8], refs[8:12])
    refs = refs[12:]
    rows, head, width = keys.shape
    span = 2 * width
    if half == 0:
        values, grad, outs, stat, bias_t, key_t, value_t, bias_n, bias_f = refs
        put_keys((keys, away), (mask[...], away[2 * rows, 0:1, :].astype(F32)), key_t, scale * LOG2E)
        put_values((values, away.at[rows : 2 * rows]), value_t)
    else:
        key_t, stat, bias_t, bias_n, bias_f = refs
    for yd, _, zd, other, slot, first in bias_pieces(at, half):
        bias_n[slot, pl.ds(first, 96), :] = pieces[other][yd][zd]
    for slot in range(2):
        for j in range(0, span, 128):
            tile = bias_n[slot, j : j + 128, :].astype(F32).T
            bias_t[slot * width : (slot + 1) * width, j : j + 128] = tile.astype(BF16)
            bias_f[slot * width : (slot + 1) * width, j : j + 128] = tile * LOG2E
    ones = rows_of((0.0, 0.0, 0.0, 1.0), 16, width).astype(BF16)

    def row_step(i, carry):
        for d in range(2):
            query = both_qg[2 * half + d, i]
            augmented = jnp.concatenate((query, query, query, ones), axis=0)
            cols = slice(d * width, (d + 1) * width)
            top, total_sum = None, None
            for k in range(0, 2 * width, 128):
                scores = dot(key_t[i, k : k + 128, :112], augmented, 1, 0)
                scores = (scores + bias_f[k : k + 128, cols]).reshape(16, 8, width)
                here = jnp.max(scores, axis=0)
                if top is None:
                    top = here
                    total_sum = jnp.sum(jnp.exp2(scores - top), axis=0)
                else:
                    new = jnp.maximum(top, here)
                    total_sum = total_sum * jnp.exp2(top - new) + jnp.sum(
                        jnp.exp2(scores - new), axis=0
                    )
                    top = new
            most = jnp.max(top, axis=0, keepdims=True)
            summed = jnp.sum(total_sum * jnp.exp2(top - most), axis=0, keepdims=True)
            stat[pl.ds(i, 1), cols] = most
            stat[pl.ds(i, 1), span + d * width : span + (d + 1) * width] = summed
        if half == 0:
            product = grad[i].astype(F32) * outs[i].astype(F32)
            stat[pl.ds(i, 1), 2 * span :] = jnp.sum(product, axis=0, keepdims=True)
        return carry

    lax.fori_loop(0, rows, row_step, 0)


def main_kernel(half, at, *refs):
    both_qg, keys, away, key_t, value_t, bias_t = refs[0:6]
    stats, first_stats = refs[6:10], refs[10:14]
    refs = refs[14:]
    rows, head, width = keys.shape
    span = 2 * width
    if half == 0:
        dk_sum, dv_sum, dq, bias_own, bias_away = refs[:5]
    else:
        dk_before, dv_before, dk_own, dv_own, dkv_away, dq, bias_own, bias_away = refs[:8]
    bias_f, acc, turned, lse, delta = refs[-5:]
    for e in range(X):
        delta[lax.rem(at[4] + e, X)] = first_stats[e][:, 2 * span :]
    tops = [stats[e][:, :span] for e in range(X)]
    sums = [stats[e][:, span : 2 * span] for e in range(X)]
    top = jnp.maximum(jnp.maximum(tops[0], tops[1]), jnp.maximum(tops[2], tops[3]))
    summed = sum(s * jnp.exp2(t - top) for s, t in zip(sums, tops))
    lse[...] = top + jnp.log(summed) * LOG2E
    bias_f[...] = bias_t[...].astype(F32) * LOG2E
    acc[...] = jnp.zeros_like(acc)

    def row_step(i, carry):
        dk_row, dv_row = None, None
        for d in range(2):
            chunk = 2 * half + d
            cols = slice(d * width, (d + 1) * width)
            query, gradient = both_qg[chunk, i], both_qg[chunk, rows + i]
            high, middle, low = split3(lse[pl.ds(i, 1), cols])
            extra = rows_of((high, middle, low, 1.0), 16, width).astype(BF16)
            query_all = jnp.concatenate((query, query, query, extra), axis=0)
            extra = rows_of(split3(delta[chunk, pl.ds(i, 1), :]), 16, width).astype(BF16)
            gradient_all = jnp.concatenate((gradient, extra), axis=0)
            probs = jnp.exp2(dot(key_t[i, :, :112], query_all, 1, 0) + bias_f[:, cols])
            dscores = probs * dot(value_t[i, :, :48], gradient_all, 1, 0)
            acc[:, cols] += dscores
            probs_low, dscores_low = probs.astype(BF16), dscores.astype(BF16)
            dv_part = dot(gradient, probs_low, 1, 1)
            dk_part = dot(query, dscores_low, 1, 1)
            dv_row = dv_part if d == 0 else dv_row + dv_part
            dk_row = dk_part if d == 0 else dk_row + dk_part
            dq_part = dot(keys[i], dscores_low[:width], 1, 0) + dot(
                away[i], dscores_low[width:], 1, 0
            )
            dq[d, i] = dq_part
        if half == 0:
            dk_sum[i], dv_sum[i] = dk_row, dv_row
        else:
            dk_row, dv_row = dk_row + dk_before[i], dv_row + dv_before[i]
            dk_own[i], dv_own[i] = dk_row[:, :width], dv_row[:, :width]
            dkv_away[i] = dk_row[:, width:].astype(BF16)
            dkv_away[rows + i] = dv_row[:, width:].astype(BF16)
        return carry

    lax.fori_loop(0, rows, row_step, 0)
    for slot in range(2):
        for j in range(0, span, 128):
            turned[slot, j : j + 128, :] = acc[slot * width : (slot + 1) * width, j : j + 128].T
    for yd, key_half, _, other, slot, first in bias_pieces(at, half):
        place = bias_own if other == 0 else bias_away
        place[yd, key_half] = turned[slot, pl.ds(first, 96), :].astype(place.dtype)


VMEM = pl.BlockSpec(memory_space=pltpu.VMEM)
SMEM = pl.BlockSpec(memory_space=pltpu.SMEM)


def call(kernel, name, args, outs, scratch, mebibytes):
    return pl.pallas_call(
        kernel,
        in_specs=[SMEM] + [VMEM] * (len(args) - 1),
        out_specs=[VMEM] * len(outs),
        out_shape=[jax.ShapeDtypeStruct(shape, dtype) for shape, dtype in outs],
        scratch_shapes=[pltpu.VMEM(shape, dtype) for shape, dtype in scratch],
        compiler_params=pltpu.CompilerParams(vmem_limit_bytes=mebibytes * 2**20),
        name=name,
    )(*args)


def fetch(x, axis, size, distance):
    return lax.ppermute(x, axis, [((n + distance) % size, n) for n in range(size)])


def deliver(x, axis, size, distance):
    return lax.ppermute(x, axis, [(n, (n + distance) % size) for n in range(size)])


def z_pairs(distance):
    pairs = []
    for group in range(ZHI):
        for place in range(ZLO):
            half, part = divmod((place + distance) % ZLO, 2)
            pairs.append(((2 * group + part) * ZHI + half, place * ZHI + group))
    return pairs


def per_device(queries, keys, values, out_grad, outputs, bias, key_mask):
    rows, head, width = keys.shape
    scale = head ** (-0.5)
    span, both = 2 * width, 2 * width
    z_axes = ("zlo", "zhi")
    at = jnp.stack([lax.axis_index(name) for name in FINE]).astype(jnp.int32)
    mask = key_mask.astype(F32)[None, :]

    both_qg = lax.all_gather(jnp.concatenate([queries, out_grad], axis=0), "x")
    from_z = jnp.stack([lax.ppermute(bias, z_axes, z_pairs(d)) for d in range(ZLO)])
    mask_rows = jnp.broadcast_to(key_mask.astype(BF16), (1, head, width))
    away = fetch(jnp.concatenate([keys, values, mask_rows], axis=0), "zhi", ZHI, 1)
    here = [from_z] + [fetch(from_z, "y", Y, d) for d in range(1, Y)]
    there = [fetch(a, "core", CORE, 1) for a in here]

    bias_shapes = [((2, span, width), BF16), ((both, span), F32)]
    transposed = ((rows, both, 128), BF16)
    stat0, bias0, key_t, value_t = call(
        lambda *refs: stats_kernel(scale, 0, *refs),
        "softmax_statistics_0",
        [at, both_qg, keys, away, mask, *here, *there, values, out_grad, outputs],
        [((rows, 2 * span + width), F32), ((both, span), BF16), transposed, transposed],
        bias_shapes,
        24,
    )
    stats0 = [stat0] + [fetch(stat0, "x", X, d) for d in range(1, X)]
    stat1, bias1 = call(
        lambda *refs: stats_kernel(scale, 1, *refs),
        "softmax_statistics_1",
        [at, both_qg, keys, away, mask, *here, *there, key_t],
        [((rows, 2 * span), F32), ((both, span), BF16)],
        bias_shapes,
        24,
    )
    stats1 = [stat1] + [fetch(stat1, "x", X, d) for d in range(1, X)]

    block, whole = ((rows, head, width), F32), ((rows, head, both), F32)
    pair, pieces = ((2, rows, head, width), F32), (Y, ZHI, 96, width)
    scratch = [
        ((both, span), F32),
        ((both, span), F32),
        ((2, span, width), F32),
        ((rows, span), F32),
        ((X, rows, width), F32),
    ]
    dk, dv, dq0, own0, away0 = call(
        lambda *refs: main_kernel(0, *refs),
        "attention_gradients_0",
        [at, both_qg, keys, away, key_t, value_t, bias0, *stats0, *stats0],
        [whole, whole, pair, (pieces, F32), (pieces, BF16)],
        scratch,
        32,
    )
    near0 = own0 + fetch(away0, "core", CORE, 1).astype(F32)
    sent0 = [near0[d].astype(BF16) for d in range(1, Y)]
    sent0, dk, dv = lax.optimization_barrier((sent0, dk, dv))
    far0 = [deliver(sent0[d - 1], "y", Y, d) for d in range(1, Y)]
    dk, dv, dkv_away, dq1, own1, away1 = call(
        lambda *refs: main_kernel(1, *refs),
        "attention_gradients_1",
        [at, both_qg, keys, away, key_t, value_t, bias1, *stats1, *stats0, dk, dv],
        [block, block, ((2 * rows, head, width), BF16), pair, (pieces, F32), (pieces, BF16)],
        scratch,
        32,
    )
    near1 = own1 + fetch(away1, "core", CORE, 1).astype(F32)
    sent1 = [near1[d].astype(BF16) for d in range(1, Y)]
    dq = jnp.concatenate([dq0, dq1], axis=0)
    sent1, dkv_away, dq = lax.optimization_barrier((sent1, dkv_away, dq))
    far1 = [deliver(sent1[d - 1], "y", Y, d) for d in range(1, Y)]

    def along_y(near, far):
        total = near[0]
        for part in far:
            total = total + part.astype(F32)
        return total.astype(BF16)

    x_at, zlo = lax.axis_index("x"), lax.axis_index("zlo")
    arrived = fetch(dkv_away, "zhi", ZHI, 1).astype(F32)
    mine = lax.dynamic_index_in_dim(dq, x_at, 0, False)
    for d in range(1, X):
        part = lax.dynamic_index_in_dim(dq, lax.rem(x_at + d, X), 0, False).astype(BF16)
        mine = mine + deliver(part, "x", X, d).astype(F32)
    low = jnp.stack([along_y(near0, far0), along_y(near1, far1)], axis=1)
    low = low.reshape(ZLO, 96, width)
    bias_grad = None
    for d in range(ZLO):
        pairs = [(worker, owner) for owner, worker in z_pairs(d)]
        part = lax.dynamic_index_in_dim(low, lax.rem(zlo + d, ZLO), 0, False)
        part = lax.ppermute(part, z_axes, pairs).astype(F32)
        bias_grad = part if bias_grad is None else bias_grad + part

    query_grad = (scale * mine).astype(BF16)
    key_grad = (scale * (dk + arrived[:rows])).astype(BF16)
    value_grad = (dv + arrived[rows:]).astype(BF16)
    return query_grad, key_grad, value_grad, bias_grad


def solution(mesh):
    fine = Mesh(mesh.devices.reshape(ZLO, Y, CORE, ZHI, X), FINE)
    row, col = ("zlo", "y", "core"), ("zhi", "x")
    pair, flat = P(row, None, col), P(row, col)
    return jax.shard_map(
        per_device,
        mesh=fine,
        in_specs=(pair,) * 5 + (flat, P(col)),
        out_specs=(pair,) * 3 + (flat,),
        check_vma=False,
    )
```

```python
import math

import jax
import jax.numpy as jnp
from jax import lax
from jax.experimental import pallas as pl
from jax.experimental.pallas import tpu as pltpu
from jax.sharding import Mesh, PartitionSpec as P

FINE = ("zlo", "y", "core", "zhi", "x")
ZLO, Y, CORE, ZHI, X = 4, 4, 2, 2, 4
LOG2E = math.log2(math.e)
MASKED = -8192.0
BF16, F32 = jnp.bfloat16, jnp.float32


def dot(a, b, ca, cb):
    return lax.dot_general(a, b, (((ca,), (cb,)), ((), ())), preferred_element_type=F32)


def split3(x):
    high = x.astype(BF16).astype(F32)
    rest = x - high
    middle = rest.astype(BF16).astype(F32)
    return high, middle, rest - middle


def rows_of(parts, count, width):
    row = lax.broadcasted_iota(jnp.int32, (count, width), 0)
    out = jnp.zeros((count, width), F32)
    for at, part in enumerate(parts):
        out = jnp.where(row == at, part, out)
    return out


def put_keys(keys, masks, place, scale):
    rows, head, width = keys[0].shape
    for slot, (ref, mask) in enumerate(zip(keys, masks)):
        offset = jnp.where(mask == 0.0, MASKED, 0.0)
        extra = rows_of((-1.0, -1.0, -1.0, offset), head, width)

        def prepare(i, carry):
            parts = split3(ref[i].astype(F32) * scale)
            whole = jnp.concatenate(parts + (extra,), axis=0)
            place[i, slot * width : (slot + 1) * width, :] = whole.T.astype(BF16)
            return carry

        lax.fori_loop(0, rows, prepare, 0)


def put_values(values, away, place):
    rows, head, width = values.shape
    extra = rows_of((-1.0, -1.0, -1.0), 128 - head, width)
    for slot, (ref, base) in enumerate(((values, 0), (away, rows))):

        def prepare(i, carry):
            whole = jnp.concatenate((ref[base + i].astype(F32), extra), axis=0)
            place[i, slot * width : (slot + 1) * width, :] = whole.T.astype(BF16)
            return carry

        lax.fori_loop(0, rows, prepare, 0)


def bias_pieces(at):
    zlo, y, core, zhi, x = (at[n] for n in range(5))
    for yd in range(Y):
        row = lax.rem(y + yd, Y)
        for zd in range(ZLO):
            piece = lax.rem(zlo + zd, ZLO)
            half, part = lax.div(piece, 2), lax.rem(piece, 2)
            slot = lax.rem(half + zhi, 2)
            chunk = lax.rem(part * 2 + lax.div(row, 2) - x + X, X)
            for other in range(CORE):
                which = lax.rem(core + other, 2)
                first = chunk * 384 + lax.rem(row, 2) * 192 + which * 96
                yield yd, zd, other, slot, pl.multiple_of(first, 32)


def stats_kernel(scale, at, *refs):
    q = refs[0:4]
    keys, away, mask, grad, outs = refs[4:9]
    pieces = (refs[9:13], refs[13:17])
    stat, bias_t = refs[17:19]
    bias_n, bias_f, key_t = refs[19:]
    rows, head, width = keys.shape
    total = X * width
    masks = (mask[...], away[2 * rows, 0:1, :].astype(F32))
    put_keys((keys, away), masks, key_t, scale * LOG2E)
    for yd, zd, other, slot, first in bias_pieces(at):
        bias_n[slot, pl.ds(first, 96), :] = pieces[other][yd][zd]
    for slot in range(2):
        for j in range(0, total, 128):
            tile = bias_n[slot, j : j + 128, :].astype(F32).T
            bias_t[slot * width : (slot + 1) * width, j : j + 128] = tile.astype(BF16)
            bias_f[slot * width : (slot + 1) * width, j : j + 128] = tile * LOG2E
    ones = rows_of((0.0, 0.0, 0.0, 1.0), 16, width).astype(BF16)

    def row_step(i, carry):
        for d in range(X):
            query = q[d][i]
            augmented = jnp.concatenate((query, query, query, ones), axis=0)
            cols = slice(d * width, (d + 1) * width)
            top, total_sum = None, None
            for k in range(0, 2 * width, 128):
                scores = dot(key_t[i, k : k + 128, :112], augmented, 1, 0)
                scores = (scores + bias_f[k : k + 128, cols]).reshape(16, 8, width)
                here = jnp.max(scores, axis=0)
                if top is None:
                    top = here
                    total_sum = jnp.sum(jnp.exp2(scores - top), axis=0)
                else:
                    new = jnp.maximum(top, here)
                    total_sum = total_sum * jnp.exp2(top - new) + jnp.sum(
                        jnp.exp2(scores - new), axis=0
                    )
                    top = new
            most = jnp.max(top, axis=0, keepdims=True)
            summed = jnp.sum(total_sum * jnp.exp2(top - most), axis=0, keepdims=True)
            stat[pl.ds(i, 1), cols] = most
            stat[pl.ds(i, 1), total + d * width : total + (d + 1) * width] = summed
        product = grad[i].astype(F32) * outs[i].astype(F32)
        stat[pl.ds(i, 1), 2 * total :] = jnp.sum(product, axis=0, keepdims=True)
        return carry

    lax.fori_loop(0, rows, row_step, 0)


def main_kernel(scale, at, *refs):
    q, (own_grad, keys, values, away, mask) = refs[0:4], refs[4:9]
    stats = refs[9:13]
    bias_t = refs[13]
    dq = refs[14:18]
    dk_own, dv_own, dkv_away, bias_own, bias_away = refs[18:23]
    bias_f, acc, turned, key_t, value_t, lse, delta = refs[23:]
    rows, head, width = keys.shape
    total = X * width
    masks = (mask[...], away[2 * rows, 0:1, :].astype(F32))
    put_keys((keys, away), masks, key_t, scale * LOG2E)
    put_values(values, away, value_t)
    for d in range(X):
        cols = slice(d * width, (d + 1) * width)
        there = [(d - e) % X for e in range(X)]
        tops = [stats[e][:, n * width : (n + 1) * width] for e, n in enumerate(there)]
        sums = [stats[e][:, total + n * width : total + (n + 1) * width] for e, n in enumerate(there)]
        top = jnp.maximum(jnp.maximum(tops[0], tops[1]), jnp.maximum(tops[2], tops[3]))
        summed = sum(s * jnp.exp2(t - top) for s, t in zip(sums, tops))
        lse[:, cols] = top + jnp.log(summed) * LOG2E
        delta[:, cols] = stats[d][:, 2 * total :]
    bias_f[...] = bias_t[...].astype(F32) * LOG2E
    acc[...] = jnp.zeros_like(acc)

    def row_step(i, carry):
        dk_row, dv_row = None, None
        for d in range(X):
            cols = slice(d * width, (d + 1) * width)
            query = q[d][i]
            gradient = own_grad[i] if d == 0 else q[d][rows + i]
            high, middle, low = split3(lse[pl.ds(i, 1), cols])
            extra = rows_of((high, middle, low, 1.0), 16, width).astype(BF16)
            query_all = jnp.concatenate((query, query, query, extra), axis=0)
            extra = rows_of(split3(delta[pl.ds(i, 1), cols]), 16, width).astype(BF16)
            gradient_all = jnp.concatenate((gradient, extra), axis=0)
            probs = jnp.exp2(dot(key_t[i, :, :112], query_all, 1, 0) + bias_f[:, cols])
            dscores = probs * dot(value_t[i, :, :48], gradient_all, 1, 0)
            acc[:, cols] += dscores
            probs_low, dscores_low = probs.astype(BF16), dscores.astype(BF16)
            dv_part = dot(gradient, probs_low, 1, 1)
            dk_part = dot(query, dscores_low, 1, 1)
            dv_row = dv_part if d == 0 else dv_row + dv_part
            dk_row = dk_part if d == 0 else dk_row + dk_part
            dq_part = dot(keys[i], dscores_low[:width], 1, 0) + dot(
                away[i], dscores_low[width:], 1, 0
            )
            dq[d][i] = dq_part.astype(dq[d].dtype)
        dk_own[i], dv_own[i] = dk_row[:, :width], dv_row[:, :width]
        dkv_away[i] = dk_row[:, width:].astype(BF16)
        dkv_away[rows + i] = dv_row[:, width:].astype(BF16)
        return carry

    lax.fori_loop(0, rows, row_step, 0)
    for slot in range(2):
        for j in range(0, total, 128):
            tile = acc[slot * width : (slot + 1) * width, j : j + 128].T
            turned[slot, j : j + 128, :] = tile
    for yd, zd, other, slot, first in bias_pieces(at):
        place = bias_own if other == 0 else bias_away
        place[yd, zd] = turned[slot, pl.ds(first, 96), :].astype(place.dtype)


VMEM = pl.BlockSpec(memory_space=pltpu.VMEM)
SMEM = pl.BlockSpec(memory_space=pltpu.SMEM)


def call(kernel, name, args, outs, scratch, mebibytes):
    return pl.pallas_call(
        kernel,
        in_specs=[SMEM] + [VMEM] * (len(args) - 1),
        out_specs=[VMEM] * len(outs),
        out_shape=[jax.ShapeDtypeStruct(shape, dtype) for shape, dtype in outs],
        scratch_shapes=[pltpu.VMEM(shape, dtype) for shape, dtype in scratch],
        compiler_params=pltpu.CompilerParams(vmem_limit_bytes=mebibytes * 2**20),
        name=name,
    )(*args)


def fetch(x, axis, size, distance):
    return lax.ppermute(x, axis, [((n + distance) % size, n) for n in range(size)])


def deliver(x, axis, size, distance):
    return lax.ppermute(x, axis, [(n, (n + distance) % size) for n in range(size)])


def z_pairs(distance):
    pairs = []
    for group in range(ZHI):
        for place in range(ZLO):
            half, part = divmod((place + distance) % ZLO, 2)
            pairs.append(((2 * group + part) * ZHI + half, place * ZHI + group))
    return pairs


def per_device(queries, keys, values, out_grad, outputs, bias, key_mask):
    rows, head, width = keys.shape
    scale = head ** (-0.5)
    total, both = X * width, 2 * width
    z_axes = ("zlo", "zhi")
    at = jnp.stack([lax.axis_index(name) for name in FINE]).astype(jnp.int32)
    mask = key_mask.astype(F32)[None, :]
    after = lax.optimization_barrier

    from_z = [lax.ppermute(bias, z_axes, z_pairs(d)) for d in range(ZLO)]
    qg = jnp.concatenate([queries, out_grad], axis=0)
    qg1 = fetch(qg, "x", X, 1)
    from_z, qg1 = after((jnp.stack(from_z), qg1))
    mask_rows = jnp.broadcast_to(key_mask.astype(BF16), (1, head, width))
    kvm = jnp.concatenate([keys, values, mask_rows], axis=0)
    kvm, qg, _ = after((kvm, qg, from_z))
    here = [from_z] + [fetch(from_z, "y", Y, d) for d in range(1, Y)]
    away = fetch(kvm, "zhi", ZHI, 1)
    qg3 = fetch(qg, "x", X, 3)
    qg, here[1] = after((qg, here[1]))
    qg2 = fetch(qg, "x", X, 2)
    there = [fetch(a, "core", CORE, 1) for a in here]
    q = [queries, qg1, qg2, qg3]

    stat, bias_t = call(
        lambda *refs: stats_kernel(scale, *refs),
        "softmax_statistics",
        [at, *q, keys, away, mask, out_grad, outputs, *here, *there],
        [((rows, 2 * total + width), F32), ((both, total), BF16)],
        [((2, total, width), BF16), ((both, total), F32), ((rows, both, 128), BF16)],
        24,
    )
    stats = [stat] + [fetch(stat, "x", X, d) for d in range(1, X)]

    block, pieces = (rows, head, width), (Y, ZLO, 96, width)
    results = call(
        lambda *refs: main_kernel(scale, *refs),
        "attention_gradients",
        [at, *q, out_grad, keys, values, away, mask, *stats, bias_t],
        [(block, F32)]
        + [(block, BF16)] * 3
        + [(block, F32)] * 2
        + [((2 * rows, head, width), BF16), (pieces, F32), (pieces, BF16)],
        [
            ((both, total), F32),
            ((both, total), F32),
            ((2, total, width), F32),
            ((rows, both, 128), BF16),
            ((rows, both, 128), BF16),
            ((rows, total), F32),
            ((rows, total), F32),
        ],
        40,
    )
    dq, (dk, dv, dkv_away, bias_own, bias_away) = results[0:4], results[4:9]

    near = bias_own + fetch(bias_away, "core", CORE, 1).astype(F32)
    arrived = fetch(dkv_away, "zhi", ZHI, 1)
    sent = [near[d].astype(BF16) for d in range(1, Y)]
    sent, dq = after((sent, dq))
    far = [deliver(sent[d - 1], "y", Y, d) for d in range(1, Y)]
    dq1 = deliver(dq[1], "x", X, 1)
    along_y = near[0]
    for part in far:
        along_y = along_y + part.astype(F32)
    low, arrived = after((along_y.astype(BF16), arrived))
    dq1, dq = after((dq1, dq))
    bias_grad = None
    for d in range(ZLO):
        pairs = [(worker, owner) for owner, worker in z_pairs(d)]
        part = lax.ppermute(low[d], z_axes, pairs).astype(F32)
        bias_grad = part if bias_grad is None else bias_grad + part

    query_sum = dq[0] + dq1.astype(F32)
    for d in (3, 2):
        query_sum = query_sum + deliver(dq[d], "x", X, d).astype(F32)
    arrived = arrived.astype(F32)
    query_grad = (scale * query_sum).astype(BF16)
    key_grad = (scale * (dk + arrived[:rows])).astype(BF16)
    value_grad = (dv + arrived[rows:]).astype(BF16)
    return query_grad, key_grad, value_grad, bias_grad


def solution(mesh):
    fine = Mesh(mesh.devices.reshape(ZLO, Y, CORE, ZHI, X), FINE)
    row, col = ("zlo", "y", "core"), ("zhi", "x")
    pair, flat = P(row, None, col), P(row, col)
    return jax.shard_map(
        per_device,
        mesh=fine,
        in_specs=(pair,) * 5 + (flat, P(col)),
        out_specs=(pair,) * 3 + (flat,),
        check_vma=False,
    )
```

```python
import math

import jax
import jax.numpy as jnp
from jax import lax
from jax.experimental import pallas as pl
from jax.experimental.pallas import tpu as pltpu
from jax.sharding import Mesh, PartitionSpec as P

FINE = ("zlo", "y", "core", "zhi", "x")
ZLO, Y, CORE, ZHI, X = 4, 4, 2, 2, 4
LOG2E = math.log2(math.e)
MASKED = -8192.0
BF16, F32 = jnp.bfloat16, jnp.float32


def dot(a, b, ca, cb):
    return lax.dot_general(a, b, (((ca,), (cb,)), ((), ())), preferred_element_type=F32)


def split3(x):
    high = x.astype(BF16).astype(F32)
    rest = x - high
    middle = rest.astype(BF16).astype(F32)
    return high, middle, rest - middle


def rows_of(parts, count, width):
    row = lax.broadcasted_iota(jnp.int32, (count, width), 0)
    out = jnp.zeros((count, width), F32)
    for at, part in enumerate(parts):
        out = jnp.where(row == at, part, out)
    return out


def put_keys(keys, masks, place, scale, start=0):
    rows, head, width = place.shape[0], *keys[0].shape[1:]
    for slot, (ref, mask) in enumerate(zip(keys, masks)):
        offset = jnp.where(mask == 0.0, MASKED, 0.0)
        extra = rows_of((-1.0, -1.0, -1.0, offset), head, width)

        def prepare(i, carry):
            parts = split3(ref[start + i].astype(F32) * scale)
            whole = jnp.concatenate(parts + (extra,), axis=0)
            place[i, slot * width : (slot + 1) * width, :] = whole.T.astype(BF16)
            return carry

        lax.fori_loop(0, rows, prepare, 0)


def put_values(values, place, start):
    rows, head, width = place.shape[0], *values[0].shape[1:]
    extra = rows_of((-1.0, -1.0, -1.0), 128 - head, width)
    for slot, ref in enumerate(values):

        def prepare(i, carry):
            whole = jnp.concatenate((ref[start + i].astype(F32), extra), axis=0)
            place[i, slot * width : (slot + 1) * width, :] = whole.T.astype(BF16)
            return carry

        lax.fori_loop(0, rows, prepare, 0)


def bias_pieces(at):
    zlo, y, core, zhi, x = (at[n] for n in range(5))
    for yd in range(Y):
        row = lax.rem(y + yd, Y)
        for zd in range(ZLO):
            piece = lax.rem(zlo + zd, ZLO)
            half, part = lax.div(piece, 2), lax.rem(piece, 2)
            slot = lax.rem(half + zhi, 2)
            chunk = lax.rem(part * 2 + lax.div(row, 2) - x + X, X)
            for other in range(CORE):
                which = lax.rem(core + other, 2)
                first = chunk * 384 + lax.rem(row, 2) * 192 + which * 96
                yield yd, zd, other, slot, pl.multiple_of(first, 32)


def stats_kernel(scale, at, *refs):
    q = refs[0:4]
    keys, away, mask, grad, outs = refs[4:9]
    pieces = (refs[9:13], refs[13:17])
    stat, bias_t = refs[17:19]
    bias_n, bias_f, key_t = refs[19:]
    rows, head, width = keys.shape
    total = X * width
    masks = (mask[...], away[rows, 0:1, :].astype(F32))
    put_keys((keys, away), masks, key_t, scale * LOG2E)
    for yd, zd, other, slot, first in bias_pieces(at):
        bias_n[slot, pl.ds(first, 96), :] = pieces[other][yd][zd]
    for slot in range(2):
        for j in range(0, total, 128):
            tile = bias_n[slot, j : j + 128, :].astype(F32).T
            bias_t[slot * width : (slot + 1) * width, j : j + 128] = tile.astype(BF16)
            bias_f[slot * width : (slot + 1) * width, j : j + 128] = tile * LOG2E
    ones = rows_of((0.0, 0.0, 0.0, 1.0), 16, width).astype(BF16)

    def row_step(i, carry):
        for d in range(X):
            query = q[d][i]
            augmented = jnp.concatenate((query, query, query, ones), axis=0)
            cols = slice(d * width, (d + 1) * width)
            top, total_sum = None, None
            for k in range(0, 2 * width, 128):
                scores = dot(key_t[i, k : k + 128, :112], augmented, 1, 0)
                scores = (scores + bias_f[k : k + 128, cols]).reshape(16, 8, width)
                here = jnp.max(scores, axis=0)
                if top is None:
                    top = here
                    total_sum = jnp.sum(jnp.exp2(scores - top), axis=0)
                else:
                    new = jnp.maximum(top, here)
                    total_sum = total_sum * jnp.exp2(top - new) + jnp.sum(
                        jnp.exp2(scores - new), axis=0
                    )
                    top = new
            most = jnp.max(top, axis=0, keepdims=True)
            summed = jnp.sum(total_sum * jnp.exp2(top - most), axis=0, keepdims=True)
            stat[pl.ds(i, 1), cols] = most + jnp.log(summed) * LOG2E
        product = grad[i].astype(F32) * outs[i].astype(F32)
        stat[pl.ds(i, 1), total:] = jnp.sum(product, axis=0, keepdims=True)
        return carry

    lax.fori_loop(0, rows, row_step, 0)


def main_kernel(scale, start, at, *refs):
    q, g = refs[0:4], refs[4:8]
    keys, values, away, away_values, mask = refs[8:13]
    stats = refs[13:17]
    bias_t = refs[17]
    refs = refs[18:]
    if start == 0:
        dq, (dk_own, dv_own, dkv_away, acc), scratch = refs[0:4], refs[4:8], refs[8:]
    else:
        acc_before, dq, refs = refs[0], refs[1:5], refs[5:]
        (dk_own, dv_own, dkv_away, bias_own, bias_away), scratch = refs[0:5], refs[5:]
        acc, turned = scratch[5:]
    bias_f, key_t, value_t, lse, delta = scratch[:5]
    rows, head, width = keys.shape
    count = key_t.shape[0]
    total = X * width
    masks = (mask[...], away[rows, 0:1, :].astype(F32))
    put_keys((keys, away), masks, key_t, scale * LOG2E, start)
    put_values((values, away_values), value_t, start)
    for d in range(X):
        cols = slice(d * width, (d + 1) * width)
        there = [(d - e) % X for e in range(X)]
        parts = [stats[e][:, n * width : (n + 1) * width] for e, n in enumerate(there)]
        top = jnp.maximum(jnp.maximum(parts[0], parts[1]), jnp.maximum(parts[2], parts[3]))
        summed = sum(jnp.exp2(part - top) for part in parts)
        lse[:, cols] = top + jnp.log(summed) * LOG2E
        delta[:, cols] = stats[d][:, total:]
    bias_f[...] = bias_t[...].astype(F32) * LOG2E
    acc[...] = jnp.zeros_like(acc) if start == 0 else acc_before[...]

    def row_step(n, carry):
        i = start + n
        dk_row, dv_row = None, None
        for d in range(X):
            cols = slice(d * width, (d + 1) * width)
            query, gradient = q[d][i], g[d][i]
            high, middle, low = split3(lse[pl.ds(i, 1), cols])
            extra = rows_of((high, middle, low, 1.0), 16, width).astype(BF16)
            query_all = jnp.concatenate((query, query, query, extra), axis=0)
            extra = rows_of(split3(delta[pl.ds(i, 1), cols]), 16, width).astype(BF16)
            gradient_all = jnp.concatenate((gradient, extra), axis=0)
            probs = jnp.exp2(dot(key_t[n, :, :112], query_all, 1, 0) + bias_f[:, cols])
            dscores = probs * dot(value_t[n, :, :48], gradient_all, 1, 0)
            acc[:, cols] += dscores
            probs_low, dscores_low = probs.astype(BF16), dscores.astype(BF16)
            dv_part = dot(gradient, probs_low, 1, 1)
            dk_part = dot(query, dscores_low, 1, 1)
            dv_row = dv_part if d == 0 else dv_row + dv_part
            dk_row = dk_part if d == 0 else dk_row + dk_part
            dq_part = dot(keys[i], dscores_low[:width], 1, 0) + dot(
                away[i], dscores_low[width:], 1, 0
            )
            dq[d][n] = dq_part.astype(dq[d].dtype)
        dk_own[n], dv_own[n] = dk_row[:, :width], dv_row[:, :width]
        dkv_away[n] = dk_row[:, width:].astype(BF16)
        dkv_away[count + n] = dv_row[:, width:].astype(BF16)
        return carry

    lax.fori_loop(0, count, row_step, 0)
    if start == 0:
        return
    for slot in range(2):
        for j in range(0, total, 128):
            tile = acc[slot * width : (slot + 1) * width, j : j + 128].T
            turned[slot, j : j + 128, :] = tile
    for yd, zd, other, slot, first in bias_pieces(at):
        place = bias_own if other == 0 else bias_away
        place[yd, zd] = turned[slot, pl.ds(first, 96), :].astype(place.dtype)


VMEM = pl.BlockSpec(memory_space=pltpu.VMEM)
SMEM = pl.BlockSpec(memory_space=pltpu.SMEM)


def call(kernel, name, args, outs, scratch, mebibytes):
    return pl.pallas_call(
        kernel,
        in_specs=[SMEM] + [VMEM] * (len(args) - 1),
        out_specs=[VMEM] * len(outs),
        out_shape=[jax.ShapeDtypeStruct(shape, dtype) for shape, dtype in outs],
        scratch_shapes=[pltpu.VMEM(shape, dtype) for shape, dtype in scratch],
        compiler_params=pltpu.CompilerParams(vmem_limit_bytes=mebibytes * 2**20),
        name=name,
    )(*args)


def fetch(x, axis, size, distance):
    return lax.ppermute(x, axis, [((n + distance) % size, n) for n in range(size)])


def deliver(x, axis, size, distance):
    return lax.ppermute(x, axis, [(n, (n + distance) % size) for n in range(size)])


def z_pairs(distance):
    pairs = []
    for group in range(ZHI):
        for place in range(ZLO):
            half, part = divmod((place + distance) % ZLO, 2)
            pairs.append(((2 * group + part) * ZHI + half, place * ZHI + group))
    return pairs


def per_device(queries, keys, values, out_grad, outputs, bias, key_mask):
    rows, head, width = keys.shape
    scale = head ** (-0.5)
    total, both = X * width, 2 * width
    z_axes = ("zlo", "zhi")
    at = jnp.stack([lax.axis_index(name) for name in FINE]).astype(jnp.int32)
    mask = key_mask.astype(F32)[None, :]
    after = lax.optimization_barrier

    from_z = [lax.ppermute(bias, z_axes, z_pairs(d)) for d in range(ZLO)]
    q1 = fetch(queries, "x", X, 1)
    from_z, q1 = after((jnp.stack(from_z), q1))
    mask_rows = jnp.broadcast_to(key_mask.astype(BF16), (1, head, width))
    km = jnp.concatenate([keys, mask_rows], axis=0)
    km, source, _ = after((km, queries, from_z))
    here = [from_z] + [fetch(from_z, "y", Y, d) for d in range(1, Y)]
    away = fetch(km, "zhi", ZHI, 1)
    q3 = fetch(source, "x", X, 3)
    source, here[1] = after((source, here[1]))
    q2 = fetch(source, "x", X, 2)
    there = [fetch(a, "core", CORE, 1) for a in here]
    grad, worth, here[1], here[2], here[3] = after((out_grad, values, *here[1:]))
    g = [fetch(grad, "x", X, d) for d in range(1, X)]
    away_values = fetch(worth, "zhi", ZHI, 1)
    q = [queries, q1, q2, q3]

    stat, bias_t = call(
        lambda *refs: stats_kernel(scale, *refs),
        "softmax_statistics",
        [at, *q, keys, away, mask, out_grad, outputs, *here, *there],
        [((rows, total + width), F32), ((both, total), BF16)],
        [((2, total, width), BF16), ((both, total), F32), ((rows, both, 128), BF16)],
        24,
    )
    stat, g, away_values = after((stat, g, away_values))
    g = [out_grad] + g
    stats = [stat] + [fetch(stat, "x", X, d) for d in range(1, X)]

    few = rows // 2
    block, pieces = (few, head, width), (Y, ZLO, 96, width)
    outs = [(block, F32)] + [(block, BF16)] * 3 + [(block, F32)] * 2
    outs = outs + [((2 * few, head, width), BF16)]
    scratch = [
        ((both, total), F32),
        ((few, both, 128), BF16),
        ((few, both, 128), BF16),
        ((rows, total), F32),
        ((rows, total), F32),
    ]
    common = [at, *q, *g, keys, values, away, away_values, mask, *stats, bias_t]
    results = call(
        lambda *refs: main_kernel(scale, 0, *refs),
        "attention_gradients_low",
        common,
        outs + [((both, total), F32)],
        scratch,
        36,
    )

    def send(results):
        dq, (dk, dv, dkv_away) = results[0:4], results[4:7]
        arrived = fetch(dkv_away, "zhi", ZHI, 1)
        return dq[0], [dq[d] for d in range(1, X)], dk, dv, arrived

    def finish(query, others, dk, dv, arrived):
        for part in others:
            query = query + part.astype(F32)
        arrived = arrived.astype(F32)
        return scale * query, scale * (dk + arrived[:few]), dv + arrived[few:]

    query0, dq0, dk0, dv0, arrived0 = send(results)
    dq0 = [deliver(dq0[d - 1], "x", X, d) for d in range(1, X)]
    results = call(
        lambda *refs: main_kernel(scale, few, *refs),
        "attention_gradients_high",
        common + [results[7]],
        outs + [(pieces, F32), (pieces, BF16)],
        scratch + [((both, total), F32), ((2, total, width), F32)],
        40,
    )
    bias_own, bias_away, dq0, arrived0 = after((results[7], results[8], dq0, arrived0))
    query1, dq1, dk1, dv1, arrived1 = send(results)
    near = bias_own + fetch(bias_away, "core", CORE, 1).astype(F32)
    sent = [near[d].astype(BF16) for d in range(1, Y)]
    far = [deliver(sent[d - 1], "y", Y, d) for d in range(1, Y)]
    far[0], dq1 = after((far[0], dq1))
    dq1 = [deliver(dq1[d - 1], "x", X, d) for d in range(1, X)]
    along_y = near[0]
    for part in far:
        along_y = along_y + part.astype(F32)
    low, arrived1 = after((along_y.astype(BF16), arrived1))
    bias_grad = None
    for d in range(ZLO):
        pairs = [(worker, owner) for owner, worker in z_pairs(d)]
        part = lax.ppermute(low[d], z_axes, pairs).astype(F32)
        bias_grad = part if bias_grad is None else bias_grad + part

    first = finish(query0, dq0, dk0, dv0, arrived0)
    second = finish(query1, dq1, dk1, dv1, arrived1)
    joined = [jnp.concatenate(pair, axis=0).astype(BF16) for pair in zip(first, second)]
    return *joined, bias_grad


def solution(mesh):
    fine = Mesh(mesh.devices.reshape(ZLO, Y, CORE, ZHI, X), FINE)
    row, col = ("zlo", "y", "core"), ("zhi", "x")
    pair, flat = P(row, None, col), P(row, col)
    return jax.shard_map(
        per_device,
        mesh=fine,
        in_specs=(pair,) * 5 + (flat, P(col)),
        out_specs=(pair,) * 3 + (flat,),
        check_vma=False,
    )
```

```python
import math

import jax
import jax.numpy as jnp
from jax import lax
from jax.experimental import pallas as pl
from jax.experimental.pallas import tpu as pltpu
from jax.sharding import Mesh, PartitionSpec as P

FINE = ("zlo", "y", "core", "zhi", "x")
ZLO, Y, CORE, ZHI, X = 4, 4, 2, 2, 4
LOG2E = math.log2(math.e)
MASKED = -8192.0
BF16, F32 = jnp.bfloat16, jnp.float32


def dot(a, b, ca, cb):
    return lax.dot_general(a, b, (((ca,), (cb,)), ((), ())), preferred_element_type=F32)


def split3(x):
    high = x.astype(BF16).astype(F32)
    rest = x - high
    middle = rest.astype(BF16).astype(F32)
    return high, middle, rest - middle


def rows_of(parts, count, width):
    row = lax.broadcasted_iota(jnp.int32, (count, width), 0)
    out = jnp.zeros((count, width), F32)
    for at, part in enumerate(parts):
        out = jnp.where(row == at, part, out)
    return out


def put_keys(keys, mask, place, first, scale):
    rows, (_, head, width) = place.shape[0], keys.shape
    extra = rows_of((-1.0, -1.0, -1.0, jnp.where(mask == 0.0, MASKED, 0.0)), head, width)

    def prepare(i, carry):
        parts = split3(keys[i].astype(F32) * scale)
        whole = jnp.concatenate(parts + (extra,), axis=0)
        place[i, first : first + width, :] = whole.T.astype(BF16)
        return carry

    lax.fori_loop(0, rows, prepare, 0)


def put_values(values, place, first):
    rows, head, width = values.shape
    extra = rows_of((-1.0, -1.0, -1.0), 128 - head, width)

    def prepare(i, carry):
        whole = jnp.concatenate((values[i].astype(F32), extra), axis=0)
        place[i, first : first + width, :] = whole.T.astype(BF16)
        return carry

    lax.fori_loop(0, rows, prepare, 0)


def prepare_kernel(scale, q, grad, outs, keys, values, mask, *made):
    qg, km, v, g, key_own, value_own, delta = made
    rows, head, width = keys.shape
    put_keys(keys, mask[...], key_own, 0, scale * LOG2E)
    put_values(values, value_own, 0)
    qg[:rows], qg[rows:], g[...] = q[...], grad[...], grad[...]
    km[:rows], v[...] = keys[...], values[...]
    km[rows] = jnp.broadcast_to(mask[...], (head, width)).astype(BF16)
    for i in range(rows):
        product = grad[i].astype(F32) * outs[i].astype(F32)
        delta[i : i + 1, :] = jnp.sum(product, axis=0, keepdims=True)


def bias_pieces(at):
    zlo, y, core, zhi, x = (at[n] for n in range(5))
    for yd in range(Y):
        row = lax.rem(y + yd, Y)
        for zd in range(ZLO):
            piece = lax.bitwise_xor(zlo, zd)
            half, part = lax.div(piece, 2), lax.rem(piece, 2)
            slot = lax.rem(half + zhi, 2)
            chunk = lax.rem(part * 2 + lax.div(row, 2) - x + X, X)
            for other in range(CORE):
                which = lax.rem(core + other, 2)
                first = chunk * 384 + lax.rem(row, 2) * 192 + which * 96
                yield yd, zd, other, slot, pl.multiple_of(first, 32)


def stats_kernel(scale, at, *refs):
    q, (away, key_own, delta) = refs[0:4], refs[4:7]
    pieces = (refs[7:11], refs[11:15])
    stat, bias_t, key_t = refs[15:18]
    bias_n, bias_f = refs[18:]
    rows, width, _ = key_own.shape
    total = X * width
    put_keys(away, away[rows, 0:1, :].astype(F32), key_t, width, scale * LOG2E)
    key_t[:, :width, :] = key_own[...]
    stat[:, total:] = delta[...]
    for yd, zd, other, slot, first in bias_pieces(at):
        bias_n[slot, pl.ds(first, 96), :] = pieces[other][yd][zd]
    for slot in range(2):
        for j in range(0, total, 128):
            tile = bias_n[slot, j : j + 128, :].astype(F32).T
            bias_t[slot * width : (slot + 1) * width, j : j + 128] = tile.astype(BF16)
            bias_f[slot * width : (slot + 1) * width, j : j + 128] = tile * LOG2E
    ones = rows_of((0.0, 0.0, 0.0, 1.0), 16, width).astype(BF16)

    def row_step(i, carry):
        for d in range(X):
            query = q[d][i]
            augmented = jnp.concatenate((query, query, query, ones), axis=0)
            cols = slice(d * width, (d + 1) * width)
            top, total_sum = None, None
            for k in range(0, 2 * width, 128):
                scores = dot(key_t[i, k : k + 128, :112], augmented, 1, 0)
                scores = (scores + bias_f[k : k + 128, cols]).reshape(16, 8, width)
                here = jnp.max(scores, axis=0)
                if top is None:
                    top = here
                    total_sum = jnp.sum(jnp.exp2(scores - top), axis=0)
                else:
                    new = jnp.maximum(top, here)
                    total_sum = total_sum * jnp.exp2(top - new) + jnp.sum(
                        jnp.exp2(scores - new), axis=0
                    )
                    top = new
            most = jnp.max(top, axis=0, keepdims=True)
            summed = jnp.sum(total_sum * jnp.exp2(top - most), axis=0, keepdims=True)
            stat[pl.ds(i, 1), cols] = most + jnp.log(summed) * LOG2E
        return carry

    lax.fori_loop(0, rows, row_step, 0)


def main_kernel(at, *refs):
    q, (g2, keys, away, away_values, key_t, value_own) = refs[0:4], refs[4:10]
    stats = refs[10:14]
    bias_t = refs[14]
    dq = refs[15:19]
    dk_own, dv_own, dkv_away, bias_own, bias_away = refs[19:24]
    bias_f, acc, turned, value_t, lse, delta = refs[24:]
    rows, head, width = away_values.shape
    total = X * width
    put_values(away_values, value_t, width)
    value_t[:, :width, :] = value_own[...]
    for d in range(X):
        cols = slice(d * width, (d + 1) * width)
        there = [(d - e) % X for e in range(X)]
        parts = [stats[e][:, n * width : (n + 1) * width] for e, n in enumerate(there)]
        top = jnp.maximum(jnp.maximum(parts[0], parts[1]), jnp.maximum(parts[2], parts[3]))
        summed = sum(jnp.exp2(part - top) for part in parts)
        lse[:, cols] = top + jnp.log(summed) * LOG2E
        delta[:, cols] = stats[d][:, total:]
    bias_f[...] = bias_t[...].astype(F32) * LOG2E
    acc[...] = jnp.zeros_like(acc)

    def row_step(i, carry):
        dk_row, dv_row = None, None
        for d in range(X):
            cols = slice(d * width, (d + 1) * width)
            query = q[d][i]
            gradient = g2[i] if d == 2 else q[d][rows + i]
            high, middle, low = split3(lse[pl.ds(i, 1), cols])
            extra = rows_of((high, middle, low, 1.0), 16, width).astype(BF16)
            query_all = jnp.concatenate((query, query, query, extra), axis=0)
            extra = rows_of(split3(delta[pl.ds(i, 1), cols]), 16, width).astype(BF16)
            gradient_all = jnp.concatenate((gradient, extra), axis=0)
            probs = jnp.exp2(dot(key_t[i, :, :112], query_all, 1, 0) + bias_f[:, cols])
            dscores = probs * dot(value_t[i, :, :48], gradient_all, 1, 0)
            acc[:, cols] += dscores
            probs_low, dscores_low = probs.astype(BF16), dscores.astype(BF16)
            dv_part = dot(gradient, probs_low, 1, 1)
            dk_part = dot(query, dscores_low, 1, 1)
            dv_row = dv_part if d == 0 else dv_row + dv_part
            dk_row = dk_part if d == 0 else dk_row + dk_part
            dq_part = dot(keys[i], dscores_low[:width], 1, 0) + dot(
                away[i], dscores_low[width:], 1, 0
            )
            dq[d][i] = dq_part.astype(dq[d].dtype)
        dk_own[i], dv_own[i] = dk_row[:, :width], dv_row[:, :width]
        dkv_away[i] = dk_row[:, width:].astype(BF16)
        dkv_away[rows + i] = dv_row[:, width:].astype(BF16)
        return carry

    lax.fori_loop(0, rows, row_step, 0)
    for slot in range(2):
        for j in range(0, total, 128):
            tile = acc[slot * width : (slot + 1) * width, j : j + 128].T
            turned[slot, j : j + 128, :] = tile
    for yd, zd, other, slot, first in bias_pieces(at):
        place = bias_own if other == 0 else bias_away
        place[yd, zd] = turned[slot, pl.ds(first, 96), :].astype(place.dtype)


VMEM = pl.BlockSpec(memory_space=pltpu.VMEM)
SMEM = pl.BlockSpec(memory_space=pltpu.SMEM)


def call(kernel, name, args, outs, scratch, mebibytes, places=1):
    return pl.pallas_call(
        kernel,
        in_specs=[SMEM] * places + [VMEM] * (len(args) - places),
        out_specs=[VMEM] * len(outs),
        out_shape=[jax.ShapeDtypeStruct(shape, dtype) for shape, dtype in outs],
        scratch_shapes=[pltpu.VMEM(shape, dtype) for shape, dtype in scratch],
        compiler_params=pltpu.CompilerParams(vmem_limit_bytes=mebibytes * 2**20),
        name=name,
    )(*args)


def fetch(x, axis, size, distance):
    return lax.ppermute(x, axis, [((n + distance) % size, n) for n in range(size)])


def deliver(x, axis, size, distance):
    return lax.ppermute(x, axis, [(n, (n + distance) % size) for n in range(size)])


def z_pairs(distance):
    pairs = []
    for group in range(ZHI):
        for place in range(ZLO):
            half, part = divmod(place ^ distance, 2)
            pairs.append(((2 * group + part) * ZHI + half, place * ZHI + group))
    return pairs


def per_device(queries, keys, values, out_grad, outputs, bias, key_mask):
    rows, head, width = keys.shape
    scale = head ** (-0.5)
    total, both = X * width, 2 * width
    z_axes = ("zlo", "zhi")
    at = jnp.stack([lax.axis_index(name) for name in FINE]).astype(jnp.int32)
    mask = key_mask.astype(F32)[None, :]
    after = lax.optimization_barrier

    from_z = [lax.ppermute(bias, z_axes, z_pairs(d)) for d in range(ZLO)]
    q2 = fetch(queries, "x", X, 2)
    block, turned = (rows, head, width), (rows, width, 128)
    made = call(
        lambda *refs: prepare_kernel(scale, *refs),
        "prepare",
        [queries, out_grad, outputs, keys, values, mask],
        [((2 * rows, head, width), BF16), ((rows + 1, head, width), BF16)]
        + [(block, BF16), (block, BF16), (turned, BF16), (turned, BF16)]
        + [((rows, width), F32)],
        [],
        16,
        0,
    )
    from_z, q2, made = after((from_z, q2, made))
    qg, km, own_values, own_grad, key_own, value_own, delta = made
    from_z = jnp.stack(from_z)
    here = [from_z] + [fetch(from_z, "y", Y, d) for d in range(1, Y)]
    qg1, qg3 = fetch(qg, "x", X, 1), fetch(qg, "x", X, 3)
    qg1, km = after((qg1, km))
    away = fetch(km, "zhi", ZHI, 1)
    there = [fetch(a, "core", CORE, 1) for a in here]
    away, own_values, own_grad = after((away, own_values, own_grad))
    away_values = fetch(own_values, "zhi", ZHI, 1)
    g2 = fetch(own_grad, "x", X, 2)
    q = [qg, qg1, q2, qg3]

    stat, bias_t, key_t = call(
        lambda *refs: stats_kernel(scale, *refs),
        "softmax_statistics",
        [at, *q, away, key_own, delta, *here, *there],
        [((rows, total + width), F32), ((both, total), BF16), ((rows, both, 128), BF16)],
        [((2, total, width), BF16), ((both, total), F32)],
        24,
    )
    stat, away_values, g2 = after((stat, away_values, g2))
    stats = [stat] + [fetch(stat, "x", X, d) for d in range(1, X)]

    pieces = (Y, ZLO, 96, width)
    results = call(
        main_kernel,
        "attention_gradients",
        [at, *q, g2, km, away, away_values, key_t, value_own, *stats, bias_t],
        [(block, F32)]
        + [(block, BF16)] * 3
        + [(block, F32)] * 2
        + [((2 * rows, head, width), BF16), (pieces, F32), (pieces, BF16)],
        [
            ((both, total), F32),
            ((both, total), F32),
            ((2, total, width), F32),
            ((rows, both, 128), BF16),
            ((rows, total), F32),
            ((rows, total), F32),
        ],
        40,
    )
    dq, (dk, dv, dkv_away, bias_own, bias_away) = results[0:4], results[4:9]

    near = bias_own + fetch(bias_away, "core", CORE, 1).astype(F32)
    arrived = fetch(dkv_away, "zhi", ZHI, 1)
    sent, first = after(([near[d].astype(BF16) for d in range(1, Y)], dq[1]))
    far = [deliver(sent[d - 1], "y", Y, d) for d in range(1, Y)]
    first = deliver(first, "x", X, 1)
    far[0], arrived, first, dq = after((far[0], arrived, first, dq))
    along_y = near[0]
    for part in far:
        along_y = along_y + part.astype(F32)
    across = [(n, n ^ 2) for n in range(ZLO)]
    kept = along_y[:2] + lax.ppermute(along_y[2:].astype(BF16), "zlo", across).astype(F32)
    bias_grad = None
    for d in range(2):
        pairs = [(worker, owner) for owner, worker in z_pairs(d)]
        part = lax.ppermute(kept[d].astype(BF16), z_axes, pairs).astype(F32)
        bias_grad = part if bias_grad is None else bias_grad + part

    query_sum = dq[0] + first.astype(F32)
    for d in range(2, X):
        query_sum = query_sum + deliver(dq[d], "x", X, d).astype(F32)
    arrived = arrived.astype(F32)
    query_grad = (scale * query_sum).astype(BF16)
    key_grad = (scale * (dk + arrived[:rows])).astype(BF16)
    value_grad = (dv + arrived[rows:]).astype(BF16)
    return query_grad, key_grad, value_grad, bias_grad


def solution(mesh):
    fine = Mesh(mesh.devices.reshape(ZLO, Y, CORE, ZHI, X), FINE)
    row, col = ("zlo", "y", "core"), ("zhi", "x")
    pair, flat = P(row, None, col), P(row, col)
    return jax.shard_map(
        per_device,
        mesh=fine,
        in_specs=(pair,) * 5 + (flat, P(col)),
        out_specs=(pair,) * 3 + (flat,),
        check_vma=False,
    )
```

```python
import math

import jax
import jax.numpy as jnp
from jax import lax
from jax.experimental import pallas as pl
from jax.experimental.pallas import tpu as pltpu
from jax.sharding import Mesh, PartitionSpec as P

FINE = ("zlo", "y", "core", "zhi", "x")
ZLO, Y, CORE, ZHI, X = 4, 4, 2, 2, 4
LOG2E = math.log2(math.e)
MASKED = -8192.0
ORDER = (0, 2, 1, 3)
BF16, F32 = jnp.bfloat16, jnp.float32


def dot(a, b, ca, cb):
    return lax.dot_general(a, b, (((ca,), (cb,)), ((), ())), preferred_element_type=F32)


def split3(x):
    high = x.astype(BF16).astype(F32)
    rest = x - high
    middle = rest.astype(BF16).astype(F32)
    return high, middle, rest - middle


def rows_of(parts, count, width):
    row = lax.broadcasted_iota(jnp.int32, (count, width), 0)
    out = jnp.zeros((count, width), F32)
    for at, part in enumerate(parts):
        out = jnp.where(row == at, part, out)
    return out


def put_keys(keys, mask, place, first, scale):
    rows, (_, head, width) = place.shape[0], keys.shape
    extra = rows_of((-1.0, -1.0, -1.0, jnp.where(mask == 0.0, MASKED, 0.0)), head, width)

    def prepare(i, carry):
        parts = split3(keys[i].astype(F32) * scale)
        whole = jnp.concatenate(parts + (extra,), axis=0)
        place[i, first : first + width, :] = whole.T.astype(BF16)
        return carry

    lax.fori_loop(0, rows, prepare, 0)


def put_values(values, place, first):
    rows, head, width = values.shape
    extra = rows_of((-1.0, -1.0, -1.0), 128 - head, width)

    def prepare(i, carry):
        whole = jnp.concatenate((values[i].astype(F32), extra), axis=0)
        place[i, first : first + width, :] = whole.T.astype(BF16)
        return carry

    lax.fori_loop(0, rows, prepare, 0)


def prepare_kernel(scale, q, grad, outs, keys, values, mask, *made):
    qg, kvm, g, key_own, value_own, delta = made
    rows, head, width = keys.shape
    put_keys(keys, mask[...], key_own, 0, scale * LOG2E)
    put_values(values, value_own, 0)
    qg[:rows], qg[rows:], g[...] = q[...], grad[...], grad[...]
    kvm[:rows], kvm[rows : 2 * rows] = keys[...], values[...]
    kvm[2 * rows] = jnp.broadcast_to(mask[...], (head, width)).astype(BF16)
    for i in range(rows):
        product = grad[i].astype(F32) * outs[i].astype(F32)
        delta[i : i + 1, :] = jnp.sum(product, axis=0, keepdims=True)


def bias_pieces(at):
    zlo, y, core, zhi, x = (at[n] for n in range(5))
    for yd in range(Y):
        row = lax.rem(y + yd, Y)
        for zd in range(ZLO):
            piece = lax.bitwise_xor(zlo, zd)
            half, part = lax.div(piece, 2), lax.rem(piece, 2)
            slot = lax.rem(half + zhi, 2)
            chunk = lax.rem(part * 2 + lax.div(row, 2) - x + X, X)
            for other in range(CORE):
                which = lax.rem(core + other, 2)
                first = chunk * 384 + lax.rem(row, 2) * 192 + which * 96
                yield yd, zd, other, slot, pl.multiple_of(first, 32)


def stats_kernel(scale, at, *refs):
    q, (away, key_own, delta) = refs[0:4], refs[4:7]
    pieces = (refs[7:11], refs[11:15])
    stat, bias_t, key_t = refs[15:18]
    bias_n, bias_f = refs[18:]
    rows, width, _ = key_own.shape
    total = X * width
    put_keys(away, away[2 * rows, 0:1, :].astype(F32), key_t, width, scale * LOG2E)
    key_t[:, :width, :] = key_own[...]
    stat[:, total:] = delta[...]
    for yd, zd, other, slot, first in bias_pieces(at):
        bias_n[slot, pl.ds(first, 96), :] = pieces[other][yd][zd]
    for slot in range(2):
        for j in range(0, total, 128):
            tile = bias_n[slot, j : j + 128, :].astype(F32).T
            bias_t[slot * width : (slot + 1) * width, j : j + 128] = tile.astype(BF16)
            bias_f[slot * width : (slot + 1) * width, j : j + 128] = tile * LOG2E
    ones = rows_of((0.0, 0.0, 0.0, 1.0), 16, width).astype(BF16)

    def row_step(i, carry):
        for d in range(X):
            query = q[d][i]
            augmented = jnp.concatenate((query, query, query, ones), axis=0)
            cols = slice(d * width, (d + 1) * width)
            top, total_sum = None, None
            for k in range(0, 2 * width, 64):
                scores = dot(key_t[i, k : k + 64, :112], augmented, 1, 0)
                scores = (scores + bias_f[k : k + 64, cols]).reshape(8, 8, width)
                here = jnp.max(scores, axis=0)
                if top is None:
                    top = here
                    total_sum = jnp.sum(jnp.exp2(scores - top), axis=0)
                else:
                    new = jnp.maximum(top, here)
                    total_sum = total_sum * jnp.exp2(top - new) + jnp.sum(
                        jnp.exp2(scores - new), axis=0
                    )
                    top = new
            most = jnp.max(top, axis=0, keepdims=True)
            summed = jnp.sum(total_sum * jnp.exp2(top - most), axis=0, keepdims=True)
            stat[pl.ds(i, 1), cols] = most + jnp.log(summed) * LOG2E
        return carry

    lax.fori_loop(0, rows, row_step, 0, unroll=2)


def main_kernel(at, *refs):
    q, (g2, keys, away, key_t, value_own) = refs[0:4], refs[4:9]
    stats = refs[9:13]
    bias_t = refs[13]
    dq = refs[14:18]
    dk_own, dv_own, dkv_away, bias_own, bias_away = refs[18:23]
    bias_f, acc, turned, value_t, lse, delta = refs[23:]
    rows, head, width = g2.shape
    total = X * width
    put_values(away.at[rows : 2 * rows], value_t, width)
    value_t[:, :width, :] = value_own[...]
    for d in range(X):
        cols = slice(d * width, (d + 1) * width)
        there = [(d - e) % X for e in range(X)]
        parts = [stats[e][:, n * width : (n + 1) * width] for e, n in enumerate(there)]
        top = jnp.maximum(jnp.maximum(parts[0], parts[1]), jnp.maximum(parts[2], parts[3]))
        summed = sum(jnp.exp2(part - top) for part in parts)
        lse[:, cols] = top + jnp.log(summed) * LOG2E
        delta[:, cols] = stats[d][:, total:]
    bias_f[...] = bias_t[...].astype(F32) * LOG2E
    acc[...] = jnp.zeros_like(acc)

    def row_step(i, carry):
        dk_row, dv_row = None, None
        both_keys = jnp.concatenate((keys[i], away[i]), axis=1)
        for d in range(X):
            cols = slice(d * width, (d + 1) * width)
            query = q[d][i]
            gradient = g2[i] if d == 2 else q[d][rows + i]
            high, middle, low = split3(lse[pl.ds(i, 1), cols])
            extra = rows_of((high, middle, low, 1.0), 16, width).astype(BF16)
            query_all = jnp.concatenate((query, query, query, extra), axis=0)
            extra = rows_of(split3(delta[pl.ds(i, 1), cols]), 16, width).astype(BF16)
            gradient_all = jnp.concatenate((gradient, extra), axis=0)
            probs = jnp.exp2(dot(key_t[i, :, :112], query_all, 1, 0) + bias_f[:, cols])
            dscores = probs * dot(value_t[i, :, :48], gradient_all, 1, 0)
            acc[:, cols] += dscores
            probs_low, dscores_low = probs.astype(BF16), dscores.astype(BF16)
            dv_part = dot(gradient, probs_low, 1, 1)
            dk_part = dot(query, dscores_low, 1, 1)
            dv_row = dv_part if d == 0 else dv_row + dv_part
            dk_row = dk_part if d == 0 else dk_row + dk_part
            dq[d][i] = dot(both_keys, dscores_low, 1, 0).astype(dq[d].dtype)
        dk_own[i], dv_own[i] = dk_row[:, :width], dv_row[:, :width]
        dkv_away[i] = dk_row[:, width:].astype(BF16)
        dkv_away[rows + i] = dv_row[:, width:].astype(BF16)
        return carry

    lax.fori_loop(0, rows, row_step, 0, unroll=2)
    for slot in range(2):
        for j in range(0, total, 128):
            tile = acc[slot * width : (slot + 1) * width, j : j + 128].T
            turned[slot, j : j + 128, :] = tile
    for yd, zd, other, slot, first in bias_pieces(at):
        place = bias_own if other == 0 else bias_away
        place[yd, ORDER[zd]] = turned[slot, pl.ds(first, 96), :].astype(place.dtype)


VMEM = pl.BlockSpec(memory_space=pltpu.VMEM)
SMEM = pl.BlockSpec(memory_space=pltpu.SMEM)


def call(kernel, name, args, outs, scratch, mebibytes, places=1):
    return pl.pallas_call(
        kernel,
        in_specs=[SMEM] * places + [VMEM] * (len(args) - places),
        out_specs=[VMEM] * len(outs),
        out_shape=[jax.ShapeDtypeStruct(shape, dtype) for shape, dtype in outs],
        scratch_shapes=[pltpu.VMEM(shape, dtype) for shape, dtype in scratch],
        compiler_params=pltpu.CompilerParams(vmem_limit_bytes=mebibytes * 2**20),
        name=name,
    )(*args)


def fetch(x, axis, size, distance):
    return lax.ppermute(x, axis, [((n + distance) % size, n) for n in range(size)])


def deliver(x, axis, size, distance):
    return lax.ppermute(x, axis, [(n, (n + distance) % size) for n in range(size)])


def z_pairs(distance):
    pairs = []
    for group in range(ZHI):
        for place in range(ZLO):
            half, part = divmod(place ^ distance, 2)
            pairs.append(((2 * group + part) * ZHI + half, place * ZHI + group))
    return pairs


def per_device(queries, keys, values, out_grad, outputs, bias, key_mask):
    rows, head, width = keys.shape
    scale = head ** (-0.5)
    total, both = X * width, 2 * width
    z_axes = ("zlo", "zhi")
    at = jnp.stack([lax.axis_index(name) for name in FINE]).astype(jnp.int32)
    mask = key_mask.astype(F32)[None, :]
    after = lax.optimization_barrier

    from_z = [lax.ppermute(bias, z_axes, z_pairs(d)) for d in range(ZLO)]
    q2 = fetch(queries, "x", X, 2)
    block, turned = (rows, head, width), (rows, width, 128)
    made = call(
        lambda *refs: prepare_kernel(scale, *refs),
        "prepare",
        [queries, out_grad, outputs, keys, values, mask],
        [((2 * rows, head, width), BF16), ((2 * rows + 1, head, width), BF16)]
        + [(block, BF16), (turned, BF16), (turned, BF16), ((rows, width), F32)],
        [],
        8,
        0,
    )
    from_z, q2, made = after((from_z, q2, made))
    qg, kvm, own_grad, key_own, value_own, delta = made
    from_z = jnp.stack(from_z)
    before, behind = fetch(from_z, "y", Y, 1), fetch(from_z, "y", Y, 3)
    qg1, qg3 = fetch(qg, "x", X, 1), fetch(qg, "x", X, 3)
    away = fetch(kvm, "zhi", ZHI, 1)
    before, qg3, source = after((before, qg3, from_z))
    here = [from_z, before, fetch(source, "y", Y, 2), behind]
    here[2], away = after((here[2], away))
    there = [fetch(a, "core", CORE, 1) for a in here]
    qg1, own_grad = after((qg1, own_grad))
    g2 = fetch(own_grad, "x", X, 2)
    q = [qg, qg1, q2, qg3]

    stat, bias_t, key_t = call(
        lambda *refs: stats_kernel(scale, *refs),
        "softmax_statistics",
        [at, *q, away, key_own, delta, *here, *there],
        [((rows, total + width), F32), ((both, total), BF16), ((rows, both, 128), BF16)],
        [((2, total, width), BF16), ((both, total), F32)],
        14,
    )
    stat, g2 = after((stat, g2))
    stats = [stat] + [fetch(stat, "x", X, d) for d in range(1, X)]

    pieces = (Y, ZLO, 96, width)
    results = call(
        main_kernel,
        "attention_gradients",
        [at, *q, g2, kvm, away, key_t, value_own, *stats, bias_t],
        [(block, F32)]
        + [(block, BF16)] * 3
        + [(block, F32)] * 2
        + [((2 * rows, head, width), BF16), (pieces, F32), (pieces, BF16)],
        [
            ((both, total), F32),
            ((both, total), F32),
            ((2, total, width), F32),
            ((rows, both, 128), BF16),
            ((rows, total), F32),
            ((rows, total), F32),
        ],
        30,
    )
    dq, (dk, dv, dkv_away, bias_own, bias_away) = results[0:4], results[4:9]

    near = bias_own + fetch(bias_away, "core", CORE, 1).astype(F32)
    arrived = fetch(dkv_away, "zhi", ZHI, 1)
    sent, first = after(([near[d].astype(BF16) for d in range(1, Y)], dq[1]))
    far = [deliver(sent[d - 1], "y", Y, d) for d in range(1, Y)]
    first = deliver(first, "x", X, 1)
    far[0], arrived, first = after((far[0], arrived, first))
    along_y = near[0]
    for part in far:
        along_y = along_y + part.astype(F32)
    along_y, dq = after((along_y, dq))
    across = [(n, n ^ 1) for n in range(ZLO)]
    kept = along_y[:2] + lax.ppermute(along_y[2:].astype(BF16), "zlo", across).astype(F32)
    bias_grad = None
    for d in range(2):
        pairs = [(worker, owner) for owner, worker in z_pairs(2 * d)]
        part = lax.ppermute(kept[d].astype(BF16), z_axes, pairs).astype(F32)
        bias_grad = part if bias_grad is None else bias_grad + part

    query_sum = dq[0] + first.astype(F32)
    for d in range(2, X):
        query_sum = query_sum + deliver(dq[d], "x", X, d).astype(F32)
    arrived = arrived.astype(F32)
    query_grad = (scale * query_sum).astype(BF16)
    key_grad = (scale * (dk + arrived[:rows])).astype(BF16)
    value_grad = (dv + arrived[rows:]).astype(BF16)
    return query_grad, key_grad, value_grad, bias_grad


def solution(mesh):
    fine = Mesh(mesh.devices.reshape(ZLO, Y, CORE, ZHI, X), FINE)
    row, col = ("zlo", "y", "core"), ("zhi", "x")
    pair, flat = P(row, None, col), P(row, col)
    return jax.shard_map(
        per_device,
        mesh=fine,
        in_specs=(pair,) * 5 + (flat, P(col)),
        out_specs=(pair,) * 3 + (flat,),
        check_vma=False,
    )
```

```python
import math

import jax
import jax.numpy as jnp
from jax import lax
from jax.experimental import pallas as pl
from jax.experimental.pallas import tpu as pltpu
from jax.sharding import Mesh, PartitionSpec as P

FINE = ("zlo", "y", "core", "zhi", "x")
ZLO, Y, CORE, ZHI, X = 4, 4, 2, 2, 4
LOG2E = math.log2(math.e)
MASKED = -8192.0
ORDER = (0, 2, 1, 3)
BF16, F32 = jnp.bfloat16, jnp.float32


def dot(a, b, ca, cb):
    return lax.dot_general(a, b, (((ca,), (cb,)), ((), ())), preferred_element_type=F32)


def split3(x):
    high = x.astype(BF16).astype(F32)
    rest = x - high
    middle = rest.astype(BF16).astype(F32)
    return high, middle, rest - middle


def rows_of(parts, count, width):
    row = lax.broadcasted_iota(jnp.int32, (count, width), 0)
    out = jnp.zeros((count, width), F32)
    for at, part in enumerate(parts):
        out = jnp.where(row == at, part, out)
    return out


def put_keys(keys, mask, place, first, scale):
    rows, (_, head, width) = place.shape[0], keys.shape
    extra = rows_of((-1.0, -1.0, -1.0, jnp.where(mask == 0.0, MASKED, 0.0)), head, width)

    def prepare(i, carry):
        parts = split3(keys[i].astype(F32) * scale)
        whole = jnp.concatenate(parts + (extra,), axis=0)
        place[i, first : first + width, :] = whole.T.astype(BF16)
        return carry

    lax.fori_loop(0, rows, prepare, 0)


def put_values(values, place, first):
    rows, head, width = values.shape
    extra = rows_of((-1.0, -1.0, -1.0), 128 - head, width)

    def prepare(i, carry):
        whole = jnp.concatenate((values[i].astype(F32), extra), axis=0)
        place[i, first : first + width, :] = whole.T.astype(BF16)
        return carry

    lax.fori_loop(0, rows, prepare, 0)


def join_kernel(q, grad, keys, values, mask, *made):
    qg, kvm, g = made
    rows, head, width = keys.shape
    qg[:rows], qg[rows:], g[...] = q[...], grad[...], grad[...]
    kvm[:rows], kvm[rows : 2 * rows] = keys[...], values[...]
    kvm[2 * rows] = jnp.broadcast_to(mask[...], (head, width)).astype(F32).astype(BF16)


def prepare_kernel(scale, qg, kvm, outs, *made):
    key_own, value_own, delta = made
    rows, head, width = outs.shape
    put_keys(kvm, kvm[2 * rows, 0:1, :].astype(F32), key_own, 0, scale * LOG2E)
    put_values(kvm.at[rows : 2 * rows], value_own, 0)
    for i in range(rows):
        product = qg[rows + i].astype(F32) * outs[i].astype(F32)
        delta[i : i + 1, :] = jnp.sum(product, axis=0, keepdims=True)


def bias_pieces(at):
    zlo, y, core, zhi, x = (at[n] for n in range(5))
    for yd in range(Y):
        row = lax.rem(y + yd, Y)
        for zd in range(ZLO):
            piece = lax.bitwise_xor(zlo, zd)
            half, part = lax.div(piece, 2), lax.rem(piece, 2)
            slot = lax.rem(half + zhi, 2)
            chunk = lax.rem(part * 2 + lax.div(row, 2) - x + X, X)
            for other in range(CORE):
                which = lax.rem(core + other, 2)
                first = chunk * 384 + lax.rem(row, 2) * 192 + which * 96
                yield yd, zd, other, slot, pl.multiple_of(first, 32)


def stats_kernel(scale, at, *refs):
    q, (away, key_own, delta) = refs[0:4], refs[4:7]
    pieces = (refs[7:11], refs[11:15])
    stat, bias_t, key_t = refs[15:18]
    bias_n, bias_f = refs[18:]
    rows, width, _ = key_own.shape
    total = X * width
    put_keys(away, away[2 * rows, 0:1, :].astype(F32), key_t, width, scale * LOG2E)
    key_t[:, :width, :] = key_own[...]
    stat[:, total:] = delta[...]
    for yd, zd, other, slot, first in bias_pieces(at):
        bias_n[slot, pl.ds(first, 96), :] = pieces[other][yd][zd]
    for slot in range(2):
        for j in range(0, total, 128):
            tile = bias_n[slot, j : j + 128, :].astype(F32).T
            bias_t[slot * width : (slot + 1) * width, j : j + 128] = tile.astype(BF16)
            bias_f[slot * width : (slot + 1) * width, j : j + 128] = tile * LOG2E
    ones = rows_of((0.0, 0.0, 0.0, 1.0), 16, width).astype(BF16)

    def row_step(i, carry):
        for d in range(X):
            query = q[d][i]
            augmented = jnp.concatenate((query, query, query, ones), axis=0)
            cols = slice(d * width, (d + 1) * width)
            top, total_sum = None, None
            for k in range(0, 2 * width, 64):
                scores = dot(key_t[i, k : k + 64, :112], augmented, 1, 0)
                scores = (scores + bias_f[k : k + 64, cols]).reshape(8, 8, width)
                here = jnp.max(scores, axis=0)
                if top is None:
                    top = here
                    total_sum = jnp.sum(jnp.exp2(scores - top), axis=0)
                else:
                    new = jnp.maximum(top, here)
                    total_sum = total_sum * jnp.exp2(top - new) + jnp.sum(
                        jnp.exp2(scores - new), axis=0
                    )
                    top = new
            most = jnp.max(top, axis=0, keepdims=True)
            summed = jnp.sum(total_sum * jnp.exp2(top - most), axis=0, keepdims=True)
            stat[pl.ds(i, 1), cols] = most + jnp.log(summed) * LOG2E
        return carry

    lax.fori_loop(0, rows, row_step, 0, unroll=2)


def main_kernel(at, *refs):
    q, (g2, keys, away, key_t, value_own) = refs[0:4], refs[4:9]
    stats = refs[9:13]
    bias_t = refs[13]
    dq = refs[14:18]
    dk_own, dv_own, dkv_away, bias_own, bias_away = refs[18:23]
    bias_f, acc, turned, value_t, lse, delta = refs[23:]
    rows, head, width = g2.shape
    total = X * width
    put_values(away.at[rows : 2 * rows], value_t, width)
    value_t[:, :width, :] = value_own[...]
    for d in range(X):
        cols = slice(d * width, (d + 1) * width)
        there = [(d - e) % X for e in range(X)]
        parts = [stats[e][:, n * width : (n + 1) * width] for e, n in enumerate(there)]
        top = jnp.maximum(jnp.maximum(parts[0], parts[1]), jnp.maximum(parts[2], parts[3]))
        summed = sum(jnp.exp2(part - top) for part in parts)
        lse[:, cols] = top + jnp.log(summed) * LOG2E
        delta[:, cols] = stats[d][:, total:]
    bias_f[...] = bias_t[...].astype(F32) * LOG2E
    acc[...] = jnp.zeros_like(acc)

    def row_step(i, carry):
        dk_row, dv_row = None, None
        both_keys = jnp.concatenate((keys[i], away[i]), axis=1)
        for d in range(X):
            cols = slice(d * width, (d + 1) * width)
            query = q[d][i]
            gradient = g2[i] if d == 2 else q[d][rows + i]
            high, middle, low = split3(lse[pl.ds(i, 1), cols])
            extra = rows_of((high, middle, low, 1.0), 16, width).astype(BF16)
            query_all = jnp.concatenate((query, query, query, extra), axis=0)
            extra = rows_of(split3(delta[pl.ds(i, 1), cols]), 16, width).astype(BF16)
            gradient_all = jnp.concatenate((gradient, extra), axis=0)
            probs = jnp.exp2(dot(key_t[i, :, :112], query_all, 1, 0) + bias_f[:, cols])
            dscores = probs * dot(value_t[i, :, :48], gradient_all, 1, 0)
            acc[:, cols] += dscores
            probs_low, dscores_low = probs.astype(BF16), dscores.astype(BF16)
            dv_part = dot(gradient, probs_low, 1, 1)
            dk_part = dot(query, dscores_low, 1, 1)
            dv_row = dv_part if d == 0 else dv_row + dv_part
            dk_row = dk_part if d == 0 else dk_row + dk_part
            dq[d][i] = dot(both_keys, dscores_low, 1, 0).astype(dq[d].dtype)
        dk_own[i], dv_own[i] = dk_row[:, :width], dv_row[:, :width]
        dkv_away[i] = dk_row[:, width:].astype(BF16)
        dkv_away[rows + i] = dv_row[:, width:].astype(BF16)
        return carry

    lax.fori_loop(0, rows, row_step, 0, unroll=2)
    for slot in range(2):
        for j in range(0, total, 128):
            tile = acc[slot * width : (slot + 1) * width, j : j + 128].T
            turned[slot, j : j + 128, :] = tile
    for yd, zd, other, slot, first in bias_pieces(at):
        place = bias_own if other == 0 else bias_away
        place[yd, ORDER[zd]] = turned[slot, pl.ds(first, 96), :].astype(place.dtype)


VMEM = pl.BlockSpec(memory_space=pltpu.VMEM)
SMEM = pl.BlockSpec(memory_space=pltpu.SMEM)


def call(kernel, name, args, outs, scratch, mebibytes, places=1):
    return pl.pallas_call(
        kernel,
        in_specs=[SMEM] * places + [VMEM] * (len(args) - places),
        out_specs=[VMEM] * len(outs),
        out_shape=[jax.ShapeDtypeStruct(shape, dtype) for shape, dtype in outs],
        scratch_shapes=[pltpu.VMEM(shape, dtype) for shape, dtype in scratch],
        compiler_params=pltpu.CompilerParams(vmem_limit_bytes=mebibytes * 2**20),
        name=name,
    )(*args)


def fetch(x, axis, size, distance):
    return lax.ppermute(x, axis, [((n + distance) % size, n) for n in range(size)])


def deliver(x, axis, size, distance):
    return lax.ppermute(x, axis, [(n, (n + distance) % size) for n in range(size)])


def z_pairs(distance):
    pairs = []
    for group in range(ZHI):
        for place in range(ZLO):
            half, part = divmod(place ^ distance, 2)
            pairs.append(((2 * group + part) * ZHI + half, place * ZHI + group))
    return pairs


def per_device(queries, keys, values, out_grad, outputs, bias, key_mask):
    rows, head, width = keys.shape
    scale = head ** (-0.5)
    total, both = X * width, 2 * width
    z_axes = ("zlo", "zhi")
    at = jnp.stack([lax.axis_index(name) for name in FINE]).astype(jnp.int32)
    after = lax.optimization_barrier

    from_z = [lax.ppermute(bias, z_axes, z_pairs(d)) for d in range(ZLO)]
    q2 = fetch(queries, "x", X, 2)
    block, turned = (rows, head, width), (rows, width, 128)
    made = call(
        join_kernel,
        "join",
        [queries, out_grad, keys, values, key_mask[None, :]],
        [((2 * rows, head, width), BF16), ((2 * rows + 1, head, width), BF16), (block, BF16)],
        [],
        6,
        0,
    )
    from_z, q2, made = after((from_z, q2, made))
    qg, kvm, own_grad = made
    made = call(
        lambda *refs: prepare_kernel(scale, *refs),
        "prepare",
        [qg, kvm, outputs],
        [(turned, BF16), (turned, BF16), ((rows, width), F32)],
        [],
        8,
        0,
    )
    from_z = jnp.stack(from_z)
    before, behind = fetch(from_z, "y", Y, 1), fetch(from_z, "y", Y, 3)
    qg1, qg3 = fetch(qg, "x", X, 1), fetch(qg, "x", X, 3)
    away = fetch(kvm, "zhi", ZHI, 1)
    before, qg3, source = after((before, qg3, from_z))
    here = [from_z, before, fetch(source, "y", Y, 2), behind]
    key_own, value_own, delta = made
    here[2], away, delta = after((here[2], away, delta))
    there = [fetch(a, "core", CORE, 1) for a in here]
    qg1, own_grad = after((qg1, own_grad))
    g2 = fetch(own_grad, "x", X, 2)
    q = [qg, qg1, q2, qg3]

    stat, bias_t, key_t = call(
        lambda *refs: stats_kernel(scale, *refs),
        "softmax_statistics",
        [at, *q, away, key_own, delta, *here, *there],
        [((rows, total + width), F32), ((both, total), BF16), ((rows, both, 128), BF16)],
        [((2, total, width), BF16), ((both, total), F32)],
        14,
    )
    stat, g2 = after((stat, g2))
    stats = [stat] + [fetch(stat, "x", X, d) for d in range(1, X)]

    pieces = (Y, ZLO, 96, width)
    results = call(
        main_kernel,
        "attention_gradients",
        [at, *q, g2, kvm, away, key_t, value_own, *stats, bias_t],
        [(block, F32)]
        + [(block, BF16)] * 3
        + [(block, F32)] * 2
        + [((2 * rows, head, width), BF16), (pieces, F32), (pieces, BF16)],
        [
            ((both, total), F32),
            ((both, total), F32),
            ((2, total, width), F32),
            ((rows, both, 128), BF16),
            ((rows, total), F32),
            ((rows, total), F32),
        ],
        30,
    )
    dq, (dk, dv, dkv_away, bias_own, bias_away) = results[0:4], results[4:9]

    near = bias_own + fetch(bias_away, "core", CORE, 1).astype(F32)
    arrived = fetch(dkv_away, "zhi", ZHI, 1)
    sent, first = after(([near[d].astype(BF16) for d in range(1, Y)], dq[1]))
    far = [deliver(sent[d - 1], "y", Y, d) for d in range(1, Y)]
    first = deliver(first, "x", X, 1)
    far[0], arrived, first = after((far[0], arrived, first))
    along_y = near[0]
    for part in far:
        along_y = along_y + part.astype(F32)
    along_y, dq = after((along_y, dq))
    across = [(n, n ^ 1) for n in range(ZLO)]
    kept = along_y[:2] + lax.ppermute(along_y[2:].astype(BF16), "zlo", across).astype(F32)
    bias_grad = None
    for d in range(2):
        pairs = [(worker, owner) for owner, worker in z_pairs(2 * d)]
        part = lax.ppermute(kept[d].astype(BF16), z_axes, pairs).astype(F32)
        bias_grad = part if bias_grad is None else bias_grad + part

    query_sum = dq[0] + first.astype(F32)
    for d in range(2, X):
        query_sum = query_sum + deliver(dq[d], "x", X, d).astype(F32)
    arrived = arrived.astype(F32)
    query_grad = (scale * query_sum).astype(BF16)
    key_grad = (scale * (dk + arrived[:rows])).astype(BF16)
    value_grad = (dv + arrived[rows:]).astype(BF16)
    return query_grad, key_grad, value_grad, bias_grad


def solution(mesh):
    fine = Mesh(mesh.devices.reshape(ZLO, Y, CORE, ZHI, X), FINE)
    row, col = ("zlo", "y", "core"), ("zhi", "x")
    pair, flat = P(row, None, col), P(row, col)
    return jax.shard_map(
        per_device,
        mesh=fine,
        in_specs=(pair,) * 5 + (flat, P(col)),
        out_specs=(pair,) * 3 + (flat,),
        check_vma=False,
    )
```

```python
import math

import jax
import jax.numpy as jnp
from jax import lax
from jax.experimental import pallas as pl
from jax.experimental.pallas import tpu as pltpu
from jax.sharding import Mesh, PartitionSpec as P

FINE = ("zlo", "y", "core", "zhi", "x")
ZLO, Y, CORE, ZHI, X = 4, 4, 2, 2, 4
LOG2E = math.log2(math.e)
MASKED = -8192.0
ORDER = (0, 2, 1, 3)
BF16, F32 = jnp.bfloat16, jnp.float32


def dot(a, b, ca, cb):
    return lax.dot_general(a, b, (((ca,), (cb,)), ((), ())), preferred_element_type=F32)


def split3(x):
    high = x.astype(BF16).astype(F32)
    rest = x - high
    middle = rest.astype(BF16).astype(F32)
    return high, middle, rest - middle


def rows_of(parts, count, width):
    row = lax.broadcasted_iota(jnp.int32, (count, width), 0)
    out = jnp.zeros((count, width), F32)
    for at, part in enumerate(parts):
        out = jnp.where(row == at, part, out)
    return out


def put_keys(keys, mask, place, first, scale):
    rows, (_, head, width) = place.shape[0], keys.shape
    extra = rows_of((-1.0, -1.0, -1.0, jnp.where(mask == 0.0, MASKED, 0.0)), head, width)

    def prepare(i, carry):
        parts = split3(keys[i].astype(F32) * scale)
        whole = jnp.concatenate(parts + (extra,), axis=0)
        place[i, first : first + width, :] = whole.T.astype(BF16)
        return carry

    lax.fori_loop(0, rows, prepare, 0)


def put_values(values, place, first):
    rows, head, width = values.shape
    extra = rows_of((-1.0, -1.0, -1.0), 128 - head, width)

    def prepare(i, carry):
        whole = jnp.concatenate((values[i].astype(F32), extra), axis=0)
        place[i, first : first + width, :] = whole.T.astype(BF16)
        return carry

    lax.fori_loop(0, rows, prepare, 0)


def join_kernel(q, grad, keys, values, mask, *made):
    qg, kvm, g = made
    rows, head, width = keys.shape
    qg[:rows], qg[rows:], g[...] = q[...], grad[...], grad[...]
    kvm[:rows], kvm[rows : 2 * rows] = keys[...], values[...]
    kvm[2 * rows] = jnp.broadcast_to(mask[...], (head, width)).astype(F32).astype(BF16)


def prepare_kernel(qg, kvm, outs, *made):
    value_own, delta = made
    rows, head, width = outs.shape
    put_values(kvm.at[rows : 2 * rows], value_own, 0)
    for i in range(rows):
        product = qg[rows + i].astype(F32) * outs[i].astype(F32)
        delta[i : i + 1, :] = jnp.sum(product, axis=0, keepdims=True)


def bias_pieces(at):
    zlo, y, core, zhi, x = (at[n] for n in range(5))
    for yd in range(Y):
        row = lax.rem(y + yd, Y)
        for zd in range(ZLO):
            piece = lax.bitwise_xor(zlo, zd)
            half, part = lax.div(piece, 2), lax.rem(piece, 2)
            slot = lax.rem(half + zhi, 2)
            chunk = lax.rem(part * 2 + lax.div(row, 2) - x + X, X)
            for other in range(CORE):
                which = lax.rem(core + other, 2)
                first = chunk * 384 + lax.rem(row, 2) * 192 + which * 96
                yield yd, zd, other, slot, pl.multiple_of(first, 32)


def stats_kernel(scale, at, *refs):
    q, (away, own, delta) = refs[0:4], refs[4:7]
    pieces = (refs[7:11], refs[11:15])
    stat, bias_t, key_t = refs[15:18]
    bias_n, bias_f = refs[18:]
    rows, width = delta.shape
    total = X * width
    put_keys(away, away[2 * rows, 0:1, :].astype(F32), key_t, width, scale * LOG2E)
    put_keys(own, own[2 * rows, 0:1, :].astype(F32), key_t, 0, scale * LOG2E)
    stat[:, total:] = delta[...]
    for yd, zd, other, slot, first in bias_pieces(at):
        bias_n[slot, pl.ds(first, 96), :] = pieces[other][yd][zd]
    for slot in range(2):
        for j in range(0, total, 128):
            tile = bias_n[slot, j : j + 128, :].astype(F32).T
            bias_t[slot * width : (slot + 1) * width, j : j + 128] = tile.astype(BF16)
            bias_f[slot * width : (slot + 1) * width, j : j + 128] = tile * LOG2E
    ones = rows_of((0.0, 0.0, 0.0, 1.0), 16, width).astype(BF16)

    def row_step(i, carry):
        for d in range(X):
            query = q[d][i]
            augmented = jnp.concatenate((query, query, query, ones), axis=0)
            cols = slice(d * width, (d + 1) * width)
            top, total_sum = None, None
            for k in range(0, 2 * width, 64):
                scores = dot(key_t[i, k : k + 64, :112], augmented, 1, 0)
                scores = (scores + bias_f[k : k + 64, cols]).reshape(8, 8, width)
                here = jnp.max(scores, axis=0)
                if top is None:
                    top = here
                    total_sum = jnp.sum(jnp.exp2(scores - top), axis=0)
                else:
                    new = jnp.maximum(top, here)
                    total_sum = total_sum * jnp.exp2(top - new) + jnp.sum(
                        jnp.exp2(scores - new), axis=0
                    )
                    top = new
            most = jnp.max(top, axis=0, keepdims=True)
            summed = jnp.sum(total_sum * jnp.exp2(top - most), axis=0, keepdims=True)
            stat[pl.ds(i, 1), cols] = most + jnp.log(summed) * LOG2E
        return carry

    lax.fori_loop(0, rows, row_step, 0, unroll=2)


def main_kernel(at, *refs):
    q, (g2, keys, away, key_t, value_own) = refs[0:4], refs[4:9]
    stats = refs[9:13]
    bias_t = refs[13]
    dq = refs[14:18]
    dk_own, dv_own, dkv_away, bias_own, bias_away = refs[18:23]
    bias_f, acc, turned, value_t, lse, delta = refs[23:]
    rows, head, width = g2.shape
    total = X * width
    put_values(away.at[rows : 2 * rows], value_t, width)
    value_t[:, :width, :] = value_own[...]
    for d in range(X):
        cols = slice(d * width, (d + 1) * width)
        there = [(d - e) % X for e in range(X)]
        parts = [stats[e][:, n * width : (n + 1) * width] for e, n in enumerate(there)]
        top = jnp.maximum(jnp.maximum(parts[0], parts[1]), jnp.maximum(parts[2], parts[3]))
        summed = sum(jnp.exp2(part - top) for part in parts)
        lse[:, cols] = top + jnp.log(summed) * LOG2E
        delta[:, cols] = stats[d][:, total:]
    bias_f[...] = bias_t[...].astype(F32) * LOG2E
    acc[...] = jnp.zeros_like(acc)

    def row_step(i, carry):
        dk_row, dv_row = None, None
        both_keys = jnp.concatenate((keys[i], away[i]), axis=1)
        for d in range(X):
            cols = slice(d * width, (d + 1) * width)
            query = q[d][i]
            gradient = g2[i] if d == 2 else q[d][rows + i]
            high, middle, low = split3(lse[pl.ds(i, 1), cols])
            extra = rows_of((high, middle, low, 1.0), 16, width).astype(BF16)
            query_all = jnp.concatenate((query, query, query, extra), axis=0)
            extra = rows_of(split3(delta[pl.ds(i, 1), cols]), 16, width).astype(BF16)
            gradient_all = jnp.concatenate((gradient, extra), axis=0)
            probs = jnp.exp2(dot(key_t[i, :, :112], query_all, 1, 0) + bias_f[:, cols])
            dscores = probs * dot(value_t[i, :, :48], gradient_all, 1, 0)
            acc[:, cols] += dscores
            probs_low, dscores_low = probs.astype(BF16), dscores.astype(BF16)
            dv_part = dot(gradient, probs_low, 1, 1)
            dk_part = dot(query, dscores_low, 1, 1)
            dv_row = dv_part if d == 0 else dv_row + dv_part
            dk_row = dk_part if d == 0 else dk_row + dk_part
            dq[d][i] = dot(both_keys, dscores_low, 1, 0).astype(dq[d].dtype)
        dk_own[i], dv_own[i] = dk_row[:, :width], dv_row[:, :width]
        dkv_away[i] = dk_row[:, width:].astype(BF16)
        dkv_away[rows + i] = dv_row[:, width:].astype(BF16)
        return carry

    lax.fori_loop(0, rows, row_step, 0, unroll=2)
    for slot in range(2):
        for j in range(0, total, 128):
            tile = acc[slot * width : (slot + 1) * width, j : j + 128].T
            turned[slot, j : j + 128, :] = tile
    for yd, zd, other, slot, first in bias_pieces(at):
        place = bias_own if other == 0 else bias_away
        place[yd, ORDER[zd]] = turned[slot, pl.ds(first, 96), :].astype(place.dtype)


VMEM = pl.BlockSpec(memory_space=pltpu.VMEM)
SMEM = pl.BlockSpec(memory_space=pltpu.SMEM)


def call(kernel, name, args, outs, scratch, mebibytes, places=1):
    return pl.pallas_call(
        kernel,
        in_specs=[SMEM] * places + [VMEM] * (len(args) - places),
        out_specs=[VMEM] * len(outs),
        out_shape=[jax.ShapeDtypeStruct(shape, dtype) for shape, dtype in outs],
        scratch_shapes=[pltpu.VMEM(shape, dtype) for shape, dtype in scratch],
        compiler_params=pltpu.CompilerParams(vmem_limit_bytes=mebibytes * 2**20),
        name=name,
    )(*args)


def fetch(x, axis, size, distance):
    return lax.ppermute(x, axis, [((n + distance) % size, n) for n in range(size)])


def deliver(x, axis, size, distance):
    return lax.ppermute(x, axis, [(n, (n + distance) % size) for n in range(size)])


def z_pairs(distance):
    pairs = []
    for group in range(ZHI):
        for place in range(ZLO):
            half, part = divmod(place ^ distance, 2)
            pairs.append(((2 * group + part) * ZHI + half, place * ZHI + group))
    return pairs


def per_device(queries, keys, values, out_grad, outputs, bias, key_mask):
    rows, head, width = keys.shape
    scale = head ** (-0.5)
    total, both = X * width, 2 * width
    z_axes = ("zlo", "zhi")
    at = jnp.stack([lax.axis_index(name) for name in FINE]).astype(jnp.int32)
    after = lax.optimization_barrier

    from_z = [lax.ppermute(bias, z_axes, z_pairs(d)) for d in range(ZLO)]
    q2 = fetch(queries, "x", X, 2)
    block, turned = (rows, head, width), (rows, width, 128)
    made = call(
        join_kernel,
        "join",
        [queries, out_grad, keys, values, key_mask[None, :]],
        [((2 * rows, head, width), BF16), ((2 * rows + 1, head, width), BF16), (block, BF16)],
        [],
        6,
        0,
    )
    from_z, q2, made = after((from_z, q2, made))
    qg, kvm, own_grad = made
    made = call(
        prepare_kernel,
        "prepare",
        [qg, kvm, outputs],
        [(turned, BF16), ((rows, width), F32)],
        [],
        8,
        0,
    )
    from_z = jnp.stack(from_z)
    before, behind = fetch(from_z, "y", Y, 1), fetch(from_z, "y", Y, 3)
    qg1, qg3 = fetch(qg, "x", X, 1), fetch(qg, "x", X, 3)
    away = fetch(kvm, "zhi", ZHI, 1)
    before, qg3, source = after((before, qg3, from_z))
    here = [from_z, before, fetch(source, "y", Y, 2), behind]
    value_own, delta = made
    here[2], away, delta = after((here[2], away, delta))
    there = [fetch(a, "core", CORE, 1) for a in here]
    qg1, own_grad = after((qg1, own_grad))
    g2 = fetch(own_grad, "x", X, 2)
    q = [qg, qg1, q2, qg3]

    stat, bias_t, key_t = call(
        lambda *refs: stats_kernel(scale, *refs),
        "softmax_statistics",
        [at, *q, away, kvm, delta, *here, *there],
        [((rows, total + width), F32), ((both, total), BF16), ((rows, both, 128), BF16)],
        [((2, total, width), BF16), ((both, total), F32)],
        14,
    )
    stat, g2 = after((stat, g2))
    stats = [stat] + [fetch(stat, "x", X, d) for d in range(1, X)]

    pieces = (Y, ZLO, 96, width)
    results = call(
        main_kernel,
        "attention_gradients",
        [at, *q, g2, kvm, away, key_t, value_own, *stats, bias_t],
        [(block, F32)]
        + [(block, BF16)] * 3
        + [(block, F32)] * 2
        + [((2 * rows, head, width), BF16), (pieces, F32), (pieces, BF16)],
        [
            ((both, total), F32),
            ((both, total), F32),
            ((2, total, width), F32),
            ((rows, both, 128), BF16),
            ((rows, total), F32),
            ((rows, total), F32),
        ],
        30,
    )
    dq, (dk, dv, dkv_away, bias_own, bias_away) = results[0:4], results[4:9]

    near = bias_own + fetch(bias_away, "core", CORE, 1).astype(F32)
    arrived = fetch(dkv_away, "zhi", ZHI, 1)
    sent, first = after(([near[d].astype(BF16) for d in range(1, Y)], dq[1]))
    far = [deliver(sent[d - 1], "y", Y, d) for d in range(1, Y)]
    first = deliver(first, "x", X, 1)
    far[0], arrived, first = after((far[0], arrived, first))
    along_y = near[0]
    for part in far:
        along_y = along_y + part.astype(F32)
    along_y, dq = after((along_y, dq))
    across = [(n, n ^ 1) for n in range(ZLO)]
    kept = along_y[:2] + lax.ppermute(along_y[2:].astype(BF16), "zlo", across).astype(F32)
    bias_grad = None
    for d in range(2):
        pairs = [(worker, owner) for owner, worker in z_pairs(2 * d)]
        part = lax.ppermute(kept[d].astype(BF16), z_axes, pairs).astype(F32)
        bias_grad = part if bias_grad is None else bias_grad + part

    query_sum = dq[0] + first.astype(F32)
    for d in range(2, X):
        query_sum = query_sum + deliver(dq[d], "x", X, d).astype(F32)
    arrived = arrived.astype(F32)
    query_grad = (scale * query_sum).astype(BF16)
    key_grad = (scale * (dk + arrived[:rows])).astype(BF16)
    value_grad = (dv + arrived[rows:]).astype(BF16)
    return query_grad, key_grad, value_grad, bias_grad


def solution(mesh):
    fine = Mesh(mesh.devices.reshape(ZLO, Y, CORE, ZHI, X), FINE)
    row, col = ("zlo", "y", "core"), ("zhi", "x")
    pair, flat = P(row, None, col), P(row, col)
    return jax.shard_map(
        per_device,
        mesh=fine,
        in_specs=(pair,) * 5 + (flat, P(col)),
        out_specs=(pair,) * 3 + (flat,),
        check_vma=False,
    )
```

```python
import math

import jax
import jax.numpy as jnp
from jax import lax
from jax.experimental import pallas as pl
from jax.experimental.pallas import tpu as pltpu
from jax.sharding import Mesh, PartitionSpec as P

FINE = ("zlo", "y", "core", "zhi", "x")
ZLO, Y, CORE, ZHI, X = 4, 4, 2, 2, 4
LOG2E = math.log2(math.e)
MASKED = -8192.0
ORDER = (0, 2, 1, 3)
BF16, F32 = jnp.bfloat16, jnp.float32


def dot(a, b, ca, cb):
    return lax.dot_general(a, b, (((ca,), (cb,)), ((), ())), preferred_element_type=F32)


def split3(x):
    high = x.astype(BF16).astype(F32)
    rest = x - high
    middle = rest.astype(BF16).astype(F32)
    return high, middle, rest - middle


def rows_of(parts, count, width):
    row = lax.broadcasted_iota(jnp.int32, (count, width), 0)
    out = jnp.zeros((count, width), F32)
    for at, part in enumerate(parts):
        out = jnp.where(row == at, part, out)
    return out


def put_keys(keys, mask, place, first, scale):
    rows, (_, head, width) = place.shape[0], keys.shape
    extra = rows_of((-1.0, -1.0, -1.0, jnp.where(mask == 0.0, MASKED, 0.0)), head, width)

    def prepare(i, carry):
        parts = split3(keys[i].astype(F32) * scale)
        whole = jnp.concatenate(parts + (extra,), axis=0)
        place[i, first : first + width, :] = whole.T.astype(BF16)
        return carry

    lax.fori_loop(0, rows, prepare, 0)


def put_values(values, place, first):
    rows, head, width = values.shape
    extra = rows_of((-1.0, -1.0, -1.0), 128 - head, width)

    def prepare(i, carry):
        whole = jnp.concatenate((values[i].astype(F32), extra), axis=0)
        place[i, first : first + width, :] = whole.T.astype(BF16)
        return carry

    lax.fori_loop(0, rows, prepare, 0)


def join_kernel(q, grad, keys, values, mask, *made):
    qg, kvm, g = made
    rows, head, width = keys.shape
    qg[:rows], qg[rows:], g[...] = q[...], grad[...], grad[...]
    kvm[:rows], kvm[rows : 2 * rows] = keys[...], values[...]
    kvm[2 * rows] = jnp.broadcast_to(mask[...], (head, width)).astype(F32).astype(BF16)


def prepare_kernel(qg, kvm, outs, *made):
    value_own, delta = made
    rows, head, width = outs.shape
    put_values(kvm.at[rows : 2 * rows], value_own, 0)
    for i in range(rows):
        product = qg[rows + i].astype(F32) * outs[i].astype(F32)
        delta[i : i + 1, :] = jnp.sum(product, axis=0, keepdims=True)


def bias_pieces(at):
    zlo, y, core, zhi, x = (at[n] for n in range(5))
    for yd in range(Y):
        row = lax.rem(y + yd, Y)
        for zd in range(ZLO):
            piece = lax.bitwise_xor(zlo, zd)
            half, part = lax.div(piece, 2), lax.rem(piece, 2)
            slot = lax.rem(half + zhi, 2)
            chunk = lax.rem(part * 2 + lax.div(row, 2) - x + X, X)
            for other in range(CORE):
                which = lax.rem(core + other, 2)
                first = chunk * 384 + lax.rem(row, 2) * 192 + which * 96
                yield yd, zd, other, slot, pl.multiple_of(first, 32)


def stats_kernel(scale, at, *refs):
    q, (away, own, delta) = refs[0:4], refs[4:7]
    pieces = (refs[7:11], refs[11:15])
    stat, bias_t, key_t = refs[15:18]
    bias_n, bias_f = refs[18:]
    rows, width = delta.shape
    total = X * width
    put_keys(away, away[2 * rows, 0:1, :].astype(F32), key_t, width, scale * LOG2E)
    put_keys(own, own[2 * rows, 0:1, :].astype(F32), key_t, 0, scale * LOG2E)
    stat[:, total:] = delta[...]
    for yd, zd, other, slot, first in bias_pieces(at):
        bias_n[slot, pl.ds(first, 96), :] = pieces[other][yd][zd]
    for slot in range(2):
        for j in range(0, total, 128):
            tile = bias_n[slot, j : j + 128, :].astype(F32).T
            bias_t[slot * width : (slot + 1) * width, j : j + 128] = tile.astype(BF16)
            bias_f[slot * width : (slot + 1) * width, j : j + 128] = tile * LOG2E
    ones = rows_of((0.0, 0.0, 0.0, 1.0), 16, width).astype(BF16)

    def row_step(i, carry):
        for d in range(X):
            query = q[d][i]
            augmented = jnp.concatenate((query, query, query, ones), axis=0)
            cols = slice(d * width, (d + 1) * width)
            top, total_sum = None, None
            for k in range(0, 2 * width, 64):
                scores = dot(key_t[i, k : k + 64, :112], augmented, 1, 0)
                scores = (scores + bias_f[k : k + 64, cols]).reshape(8, 8, width)
                here = jnp.max(scores, axis=0)
                if top is None:
                    top = here
                    total_sum = jnp.sum(jnp.exp2(scores - top), axis=0)
                else:
                    new = jnp.maximum(top, here)
                    total_sum = total_sum * jnp.exp2(top - new) + jnp.sum(
                        jnp.exp2(scores - new), axis=0
                    )
                    top = new
            most = jnp.max(top, axis=0, keepdims=True)
            summed = jnp.sum(total_sum * jnp.exp2(top - most), axis=0, keepdims=True)
            stat[pl.ds(i, 1), cols] = most + jnp.log(summed) * LOG2E
        return carry

    lax.fori_loop(0, rows, row_step, 0, unroll=4)


def main_kernel(at, *refs):
    q, (g2, keys, away, key_t, value_own) = refs[0:4], refs[4:9]
    stats = refs[9:13]
    bias_t = refs[13]
    dq = refs[14:18]
    dk_own, dv_own, dkv_away, bias_own, bias_away = refs[18:23]
    bias_f, acc, turned, value_t, lse, delta = refs[23:]
    rows, head, width = g2.shape
    total = X * width
    put_values(away.at[rows : 2 * rows], value_t, width)
    value_t[:, :width, :] = value_own[...]
    for d in range(X):
        cols = slice(d * width, (d + 1) * width)
        there = [(d - e) % X for e in range(X)]
        parts = [stats[e][:, n * width : (n + 1) * width] for e, n in enumerate(there)]
        top = jnp.maximum(jnp.maximum(parts[0], parts[1]), jnp.maximum(parts[2], parts[3]))
        summed = sum(jnp.exp2(part - top) for part in parts)
        lse[:, cols] = top + jnp.log(summed) * LOG2E
        delta[:, cols] = stats[d][:, total:]
    bias_f[...] = bias_t[...].astype(F32) * LOG2E
    acc[...] = jnp.zeros_like(acc)

    def row_step(i, carry):
        dk_row, dv_row = None, None
        both_keys = jnp.concatenate((keys[i], away[i]), axis=1)
        for d in range(X):
            cols = slice(d * width, (d + 1) * width)
            query = q[d][i]
            gradient = g2[i] if d == 2 else q[d][rows + i]
            high, middle, low = split3(lse[pl.ds(i, 1), cols])
            extra = rows_of((high, middle, low, 1.0), 16, width).astype(BF16)
            query_all = jnp.concatenate((query, query, query, extra), axis=0)
            extra = rows_of(split3(delta[pl.ds(i, 1), cols]), 16, width).astype(BF16)
            gradient_all = jnp.concatenate((gradient, extra), axis=0)
            probs = jnp.exp2(dot(key_t[i, :, :112], query_all, 1, 0) + bias_f[:, cols])
            dscores = probs * dot(value_t[i, :, :48], gradient_all, 1, 0)
            acc[:, cols] += dscores
            probs_low, dscores_low = probs.astype(BF16), dscores.astype(BF16)
            dv_part = dot(gradient, probs_low, 1, 1)
            dk_part = dot(query, dscores_low, 1, 1)
            dv_row = dv_part if d == 0 else dv_row + dv_part
            dk_row = dk_part if d == 0 else dk_row + dk_part
            dq[d][i] = dot(both_keys, dscores_low, 1, 0).astype(dq[d].dtype)
        dk_own[i], dv_own[i] = dk_row[:, :width], dv_row[:, :width]
        dkv_away[i] = dk_row[:, width:].astype(BF16)
        dkv_away[rows + i] = dv_row[:, width:].astype(BF16)
        return carry

    lax.fori_loop(0, rows, row_step, 0, unroll=2)
    for slot in range(2):
        for j in range(0, total, 128):
            tile = acc[slot * width : (slot + 1) * width, j : j + 128].T
            turned[slot, j : j + 128, :] = tile
    for yd, zd, other, slot, first in bias_pieces(at):
        place = bias_own if other == 0 else bias_away
        place[yd, ORDER[zd]] = turned[slot, pl.ds(first, 96), :].astype(place.dtype)


VMEM = pl.BlockSpec(memory_space=pltpu.VMEM)
SMEM = pl.BlockSpec(memory_space=pltpu.SMEM)


def call(kernel, name, args, outs, scratch, mebibytes, places=1):
    return pl.pallas_call(
        kernel,
        in_specs=[SMEM] * places + [VMEM] * (len(args) - places),
        out_specs=[VMEM] * len(outs),
        out_shape=[jax.ShapeDtypeStruct(shape, dtype) for shape, dtype in outs],
        scratch_shapes=[pltpu.VMEM(shape, dtype) for shape, dtype in scratch],
        compiler_params=pltpu.CompilerParams(vmem_limit_bytes=mebibytes * 2**20),
        name=name,
    )(*args)


def fetch(x, axis, size, distance):
    return lax.ppermute(x, axis, [((n + distance) % size, n) for n in range(size)])


def deliver(x, axis, size, distance):
    return lax.ppermute(x, axis, [(n, (n + distance) % size) for n in range(size)])


def z_pairs(distance):
    pairs = []
    for group in range(ZHI):
        for place in range(ZLO):
            half, part = divmod(place ^ distance, 2)
            pairs.append(((2 * group + part) * ZHI + half, place * ZHI + group))
    return pairs


def per_device(queries, keys, values, out_grad, outputs, bias, key_mask):
    rows, head, width = keys.shape
    scale = head ** (-0.5)
    total, both = X * width, 2 * width
    z_axes = ("zlo", "zhi")
    at = jnp.stack([lax.axis_index(name) for name in FINE]).astype(jnp.int32)
    after = lax.optimization_barrier

    from_z = [lax.ppermute(bias, z_axes, z_pairs(d)) for d in range(ZLO)]
    q2 = fetch(queries, "x", X, 2)
    block, turned = (rows, head, width), (rows, width, 128)
    made = call(
        join_kernel,
        "join",
        [queries, out_grad, keys, values, key_mask[None, :]],
        [((2 * rows, head, width), BF16), ((2 * rows + 1, head, width), BF16), (block, BF16)],
        [],
        6,
        0,
    )
    from_z, q2, made = after((from_z, q2, made))
    qg, kvm, own_grad = made
    made = call(
        prepare_kernel,
        "prepare",
        [qg, kvm, outputs],
        [(turned, BF16), ((rows, width), F32)],
        [],
        8,
        0,
    )
    from_z = jnp.stack(from_z)
    before, behind = fetch(from_z, "y", Y, 1), fetch(from_z, "y", Y, 3)
    qg1, qg3 = fetch(qg, "x", X, 1), fetch(qg, "x", X, 3)
    away = fetch(kvm, "zhi", ZHI, 1)
    before, qg3, source = after((before, qg3, from_z))
    here = [from_z, before, fetch(source, "y", Y, 2), behind]
    value_own, delta = made
    here[2], away, delta = after((here[2], away, delta))
    there = [fetch(a, "core", CORE, 1) for a in here]
    qg1, own_grad = after((qg1, own_grad))
    g2 = fetch(own_grad, "x", X, 2)
    q = [qg, qg1, q2, qg3]

    stat, bias_t, key_t = call(
        lambda *refs: stats_kernel(scale, *refs),
        "softmax_statistics",
        [at, *q, away, kvm, delta, *here, *there],
        [((rows, total + width), F32), ((both, total), BF16), ((rows, both, 128), BF16)],
        [((2, total, width), BF16), ((both, total), F32)],
        14,
    )
    stat, g2 = after((stat, g2))
    stats = [stat] + [fetch(stat, "x", X, d) for d in range(1, X)]

    pieces = (Y, ZLO, 96, width)
    results = call(
        main_kernel,
        "attention_gradients",
        [at, *q, g2, kvm, away, key_t, value_own, *stats, bias_t],
        [(block, F32)]
        + [(block, BF16)] * 3
        + [(block, F32)] * 2
        + [((2 * rows, head, width), BF16), (pieces, F32), (pieces, BF16)],
        [
            ((both, total), F32),
            ((both, total), F32),
            ((2, total, width), F32),
            ((rows, both, 128), BF16),
            ((rows, total), F32),
            ((rows, total), F32),
        ],
        30,
    )
    dq, (dk, dv, dkv_away, bias_own, bias_away) = results[0:4], results[4:9]

    near = bias_own + fetch(bias_away, "core", CORE, 1).astype(F32)
    arrived = fetch(dkv_away, "zhi", ZHI, 1)
    sent, first = after(([near[d].astype(BF16) for d in range(1, Y)], dq[1]))
    far = [deliver(sent[d - 1], "y", Y, d) for d in range(1, Y)]
    first = deliver(first, "x", X, 1)
    far[0], arrived, first = after((far[0], arrived, first))
    along_y = near[0]
    for part in far:
        along_y = along_y + part.astype(F32)
    along_y, dq = after((along_y, dq))
    across = [(n, n ^ 1) for n in range(ZLO)]
    kept = along_y[:2] + lax.ppermute(along_y[2:].astype(BF16), "zlo", across).astype(F32)
    bias_grad = None
    for d in range(2):
        pairs = [(worker, owner) for owner, worker in z_pairs(2 * d)]
        part = lax.ppermute(kept[d].astype(BF16), z_axes, pairs).astype(F32)
        bias_grad = part if bias_grad is None else bias_grad + part

    query_sum = dq[0] + first.astype(F32)
    for d in range(2, X):
        query_sum = query_sum + deliver(dq[d], "x", X, d).astype(F32)
    arrived = arrived.astype(F32)
    query_grad = (scale * query_sum).astype(BF16)
    key_grad = (scale * (dk + arrived[:rows])).astype(BF16)
    value_grad = (dv + arrived[rows:]).astype(BF16)
    return query_grad, key_grad, value_grad, bias_grad


def solution(mesh):
    fine = Mesh(mesh.devices.reshape(ZLO, Y, CORE, ZHI, X), FINE)
    row, col = ("zlo", "y", "core"), ("zhi", "x")
    pair, flat = P(row, None, col), P(row, col)
    return jax.shard_map(
        per_device,
        mesh=fine,
        in_specs=(pair,) * 5 + (flat, P(col)),
        out_specs=(pair,) * 3 + (flat,),
        check_vma=False,
    )
```
